512 devices in a mesh: ctx: 16 (over z_hi, y, core), zero: 32 (over z_lo, x).
Axes of the slice: x: 4, y: 4, z: 16 (z_hi: 2, z_lo: 8; z = z_hi * 8 + z_lo), core: 2. Of those that a mesh axis runs over, the one named last changes fastest.
Arguments:
- tokens: bfloat16 [65536, 2048], P(('ctx', 'zero')), may hold values from -6 to 6
- in_weight: bfloat16 [3, 2048, 2048], P(None, 'zero', 'ctx'), may hold values from -0.125 to 0.125
- filters: float32 [128, 128], P('ctx'), may hold values from -1 to 1
- doc_offset: int32 [16, 4096], P(None, 'zero'), may hold values from 0 to 1023, as said below
- cotangent: bfloat16 [65536, 2048], P(('ctx', 'zero')), may hold values from -6 to 6
Outputs:
- gated_out: bfloat16 [65536, 2048], P(('ctx', 'zero'))
- grad_in_weight: float32 [3, 2048, 2048], P(None, 'zero', 'ctx')
- grad_filters: float32 [128, 128], P('ctx')
The draws below stay inside these ranges and needn't reach their ends.
Inputs may be any that keep to these rules, and one draw needn't show every extreme that they name: `doc_offset`: offset from the document's first token; offsets rise by one along the sequence and restart at 0 where a document begins; every document has at most 1024 tokens and the first has exactly 1024.
All inputs are finite; a program needn't handle non-finite values.
Results may differ from the reference program's by a relative error of at most 0.033.
Values may be sent and summed in bfloat16 or wider, within the bound.
No kernel may reach another device: no remote copies, remote signals or barrier semaphores. Data moves between devices by JAX's collectives and lax.ppermute only.
A program may use at most 128 MiB of HBM per device.

```python
import math
from functools import partial
import jax
import jax.numpy as jnp
from jax import lax

D = 2048
C = 2048
GSIZE = 16
TAPS = 128
TOK_DEV = 128
TOKENS = 65536
GROUPS = 128
MOST_DOC = 1024
N_CTX = 16
N_ZERO = 32


def draw_filters(key, part):
    key = jax.random.fold_in(key, 5)
    rate_key, random_key = jax.random.split(key)
    tap_lag = jnp.arange(TAPS, dtype=jnp.float32)
    decay_rate = jnp.exp(jax.random.uniform(rate_key, (GROUPS, 1), jnp.float32, math.log(1.0 / (4.0 * TAPS)), math.log(1.0 / 12.0)))
    random_taps = jnp.clip(jax.random.normal(random_key, (GROUPS, TAPS), jnp.float32), -4.0, 4.0)
    return random_taps * jnp.exp(-decay_rate * tap_lag[None, :]) * 0.25


def draw_doc_offset(key, part):
    key = jax.random.fold_in(key, 11)
    positions = jnp.arange(TOKENS, dtype=jnp.int32)
    starts = jax.random.randint(key, (TOKENS,), 0, 2 * TOK_DEV) == 0
    forced = (positions % MOST_DOC == MOST_DOC // 2) | (positions == MOST_DOC)
    starts = (starts | forced) & ((positions >= MOST_DOC) | (positions == 0))
    doc_begin = lax.cummax(jnp.where(starts, positions, 0), axis=0)
    return (positions - doc_begin).reshape(N_CTX, N_ZERO * TOK_DEV)


def block_scale(own_key, shape, shards, least, high):
    factor_of, own = 1.0, jax.random.fold_in(own_key, 6)
    for axis_at, parts in shards:
        steps = jnp.exp(jax.random.uniform(jax.random.fold_in(own, axis_at), (parts,), jnp.float32, least / len(shards), high / len(shards)))
        factor_of = factor_of * jnp.repeat(steps, shape[axis_at] // parts).reshape([-1 if axis == axis_at else 1 for axis in range(len(shape))])
    return factor_of


def normal_values(stream_key, extent, width, most, pieces=(), kind=jnp.bfloat16):
    drawn = width * jax.random.normal(stream_key, extent, jnp.float32)
    if pieces:
        drawn = drawn * block_scale(stream_key, extent, pieces, -0.22, 0.18)
    return jnp.clip(drawn, -most, most).astype(kind)


def setup_inputs(seed: int = 0) -> dict:
    key_list = jax.random.split(jax.random.key(seed), 6)
    return {
        "tokens": normal_values(key_list[0], (TOKENS, D), 1.0, 6.0, ((0, 512),)),
        "in_weight": normal_values(key_list[1], (3, D, C), D ** -0.5, 0.125, ((1, 32), (2, 16))),
        "filters": draw_filters(jax.random.fold_in(key_list[5], 71), 0),
        "doc_offset": draw_doc_offset(jax.random.fold_in(key_list[5], 71), 0),
        "cotangent": normal_values(key_list[4], (TOKENS, C), 1.0, 6.0, ((0, 512),)),
    }


def channel_block(tokens, offset, block_args):
    weights_blk, filter_blk, cotangent_blk = block_args
    tap_count = filter_blk.shape[1]
    total_rows = tokens.shape[0]
    col_width = weights_blk.shape[2]
    queries = jnp.dot(tokens, weights_blk[0], preferred_element_type=jnp.float32).astype(jnp.bfloat16)
    key_part = jnp.dot(tokens, weights_blk[1], preferred_element_type=jnp.float32).astype(jnp.bfloat16)
    values = jnp.dot(tokens, weights_blk[2], preferred_element_type=jnp.float32).astype(jnp.bfloat16)
    product = (key_part.astype(jnp.float32) * values.astype(jnp.float32)).astype(jnp.bfloat16)
    channel_taps = jnp.repeat(filter_blk, GSIZE, axis=0).T
    padded = jnp.concatenate([jnp.zeros((tap_count - 1, col_width), jnp.float32), product.astype(jnp.float32)], 0)

    def forward_tap(tap_index, running):
        tap_index = jnp.asarray(tap_index).astype(jnp.int32)
        window = lax.dynamic_slice_in_dim(padded, (tap_count - 1 - tap_index).astype(jnp.int32), total_rows, 0)
        reach = (offset >= tap_index)[:, None]
        return running + jnp.where(reach, channel_taps[tap_index][None, :] * window, jnp.float32(0.0))

    mixed = lax.fori_loop(0, tap_count, forward_tap, jnp.zeros((total_rows, col_width), jnp.float32))
    gated_out = (queries.astype(jnp.float32) * mixed).astype(jnp.bfloat16)
    cotangent_f = cotangent_blk.astype(jnp.float32)
    grad_query = cotangent_f * mixed
    grad_mixed = cotangent_f * queries.astype(jnp.float32)
    trailing = jnp.zeros((tap_count - 1, col_width), jnp.float32)

    def backward_tap(tap_index, carry):
        grad_product, grad_taps = carry
        tap_index = jnp.asarray(tap_index).astype(jnp.int32)
        masked = jnp.where((offset >= tap_index)[:, None], grad_mixed, jnp.float32(0.0))
        lowered = jnp.concatenate([masked, trailing], 0)
        moved = lax.dynamic_slice_in_dim(lowered, tap_index, total_rows, 0)
        grad_product = grad_product + channel_taps[tap_index][None, :] * moved
        window = lax.dynamic_slice_in_dim(padded, (tap_count - 1 - tap_index).astype(jnp.int32), total_rows, 0)
        grad_taps = grad_taps.at[tap_index].set(jnp.sum(masked * window, axis=0))
        return grad_product, grad_taps

    grad_product, grad_taps = lax.fori_loop(
        0, tap_count, backward_tap,
        (jnp.zeros((total_rows, col_width), jnp.float32), jnp.zeros((tap_count, col_width), jnp.float32)))
    grad_filter = grad_taps.reshape(tap_count, col_width // GSIZE, GSIZE).sum(axis=2).T
    grad_key = grad_product * values.astype(jnp.float32)
    grad_value = grad_product * key_part.astype(jnp.float32)
    grads = jnp.stack([grad_query, grad_key, grad_value]).astype(jnp.bfloat16)
    tokens_t = tokens.T
    grad_weight = jnp.stack([jnp.dot(tokens_t, grads[p], preferred_element_type=jnp.float32) for p in range(3)])
    return gated_out, grad_weight, grad_filter


def reference(tokens, in_weight, filters, doc_offset, cotangent):
    col_width = C // N_CTX
    offset = doc_offset.reshape(TOKENS)
    weight_blocks = in_weight.reshape(3, D, N_CTX, col_width).transpose(2, 0, 1, 3)
    filter_blocks = filters.reshape(N_CTX, GROUPS // N_CTX, TAPS)
    cotangent_blocks = cotangent.reshape(TOKENS, N_CTX, col_width).transpose(1, 0, 2)
    gated, grad_weight, grad_filter = lax.map(partial(channel_block, tokens, offset),
                                             (weight_blocks, filter_blocks, cotangent_blocks))
    gated_out = gated.transpose(1, 0, 2).reshape(TOKENS, C)
    grad_in_weight = grad_weight.transpose(1, 2, 0, 3).reshape(3, D, C)
    grad_filters = grad_filter.reshape(GROUPS, TAPS)
    return gated_out, grad_in_weight, grad_filters
```

```python
import jax
import jax.numpy as jnp
from jax import lax
from jax.experimental import pallas as pl
from jax.experimental.pallas import tpu as pltpu
from jax.sharding import Mesh, PartitionSpec as P

BF = jnp.bfloat16
F32 = jnp.float32
LANES = 128
GSIZE = 16
PER = LANES // GSIZE
CTX = ("z_hi", "y", "core")
ZERO = ("z_lo", "x")
TOK_AX = ("y", "core")
Z_AX = ("z_hi", "z_lo")
SEQ_AX = ("z_hi", "z_lo", "x")


def swap_blocks(pieces, axes):
    return lax.all_to_all(pieces, axes, split_axis=0, concat_axis=0, tiled=True)


def spread(shard, axes):
    count = lax.axis_size(axes)
    return swap_blocks(jnp.broadcast_to(shard[None], (count,) + shard.shape), axes)


def iotas():
    rows = lax.broadcasted_iota(jnp.int32, (LANES, LANES), 0)
    cols = lax.broadcasted_iota(jnp.int32, (LANES, LANES), 1)
    return rows, cols


def group_lanes(block, g):
    lane = lax.broadcasted_iota(jnp.int32, block.shape, 1)
    return jnp.where(lane // GSIZE == g, block, jnp.zeros_like(block))


def circulants(taps_ref, table_ref):
    for g in range(taps_ref.shape[0]):
        rows = jnp.broadcast_to(taps_ref[g : g + 1, :], (LANES, LANES))
        table_ref[g] = pltpu.roll(rows, 0, 1, stride=1, stride_axis=0).astype(BF)


def back_kernel(off_ref, taps_ref, q_ref, cot_ref, prev_ref, own_ref, table):
    @pl.when(pl.program_id(0) == 0)
    def _():
        circulants(taps_ref, table)

    u, t = iotas()
    off = jnp.broadcast_to(off_ref[0], (LANES, LANES))
    lag = t - u
    m_own = jnp.where((lag >= 0) & (lag <= off), 1.0, 0.0).astype(BF)
    m_prev = jnp.where((lag < 0) & (lag + LANES <= off), 1.0, 0.0).astype(BF)
    grad = (cot_ref[0].astype(F32) * q_ref[0].astype(F32)).astype(BF)
    for half in range(grad.shape[1] // LANES):
        cols = slice(half * LANES, (half + 1) * LANES)
        g_half = grad[:, cols]
        right = jnp.concatenate([group_lanes(g_half, g) for g in range(PER)], 0)
        tabs = [table[half * PER + g] for g in range(PER)]
        prev = jnp.concatenate([tab * m_prev for tab in tabs], 1)
        own = jnp.concatenate([tab * m_own for tab in tabs], 1)
        prev_ref[0, :, cols] = jnp.dot(prev, right, preferred_element_type=F32).astype(BF)
        own_ref[0, :, cols] = jnp.dot(own, right, preferred_element_type=F32)


def front_kernel(off_ref, taps_ref, q_ref, cot_ref, prod_ref, halo_ref, gated_ref, gq_ref, df_ref, table, acc):
    step = pl.program_id(0)

    @pl.when(step == 0)
    def _():
        circulants(taps_ref, table)
        acc[...] = jnp.zeros_like(acc)

    t, u = iotas()
    off = jnp.broadcast_to(off_ref[0], (LANES, LANES)).T
    lag = t - u
    is_own = (lag >= 0) & (lag <= off)
    is_prev = (lag < 0) & (lag + LANES <= off)
    m_own = jnp.where(is_own, 1.0, 0.0).astype(BF)
    m_prev = jnp.where(is_prev, 1.0, 0.0).astype(BF)
    q = q_ref[0].astype(F32)
    cot = cot_ref[0].astype(F32)
    grad = (cot * q).astype(BF)
    for half in range(grad.shape[1] // LANES):
        cols = slice(half * LANES, (half + 1) * LANES)
        ext = jnp.concatenate([halo_ref[0, :, cols], prod_ref[0, :, cols]], 0)
        right = jnp.concatenate([group_lanes(ext, g) for g in range(PER)], 0)
        left = []
        for g in range(PER):
            tab = table[half * PER + g]
            left += [tab * m_prev, tab * m_own]
        mixed = jnp.dot(jnp.concatenate(left, 1), right, preferred_element_type=F32)
        gated_ref[0, :, cols] = (q[:, cols] * mixed).astype(BF)
        gq_ref[0, :, cols] = (cot[:, cols] * mixed).astype(BF)
        g_half = grad[:, cols]
        rows = jnp.concatenate([group_lanes(g_half, g) for g in range(PER)], 0)
        sums = lax.dot_general(rows, ext, (((1,), (1,)), ((), ())), preferred_element_type=F32)
        for g in range(PER):
            part = sums[g * LANES : (g + 1) * LANES]
            picked = jnp.where(is_own, part[:, LANES:], jnp.where(is_prev, part[:, :LANES], 0.0))
            acc[half * PER + g] += picked

    @pl.when(step == pl.num_programs(0) - 1)
    def _():
        for g in range(acc.shape[0]):
            lined = acc[g]
            for bit in range(7):
                turned = pltpu.roll(lined, LANES - (1 << bit), 1)
                lined = jnp.where((t >> bit) & 1 == 1, turned, lined)
            df_ref[g : g + 1, :] = jnp.sum(lined, axis=0, keepdims=True)


def block_spec(width):
    return pl.BlockSpec((1, LANES, width), lambda i: (i, 0, 0))


def whole_spec(shape):
    return pl.BlockSpec(shape, lambda i: (0,) * len(shape))


PARAMS = pltpu.CompilerParams(dimension_semantics=("arbitrary",), vmem_limit_bytes=40 << 20)


def back(off, taps, q, cot):
    n, _, width = q.shape
    groups = taps.shape[0]
    off_spec = pl.BlockSpec((1, 1, LANES), lambda i: (i, 0, 0))
    flops = 2 * n * 2 * LANES * LANES * PER * width
    return pl.pallas_call(
        back_kernel,
        grid=(n,),
        in_specs=[off_spec, whole_spec(taps.shape), block_spec(width), block_spec(width)],
        out_specs=[block_spec(width), block_spec(width)],
        out_shape=[jax.ShapeDtypeStruct(q.shape, BF), jax.ShapeDtypeStruct(q.shape, F32)],
        scratch_shapes=[pltpu.VMEM((groups, LANES, LANES), BF)],
        compiler_params=PARAMS,
        cost_estimate=pl.CostEstimate(flops=flops, bytes_accessed=10 * q.size, transcendentals=0),
    )(off, taps, q, cot)


def front(off, taps, q, cot, product, halo):
    n, _, width = q.shape
    groups = taps.shape[0]
    off_spec = pl.BlockSpec((1, 1, LANES), lambda i: (i, 0, 0))
    flops = 4 * n * 2 * LANES * LANES * PER * width
    return pl.pallas_call(
        front_kernel,
        grid=(n,),
        in_specs=[off_spec, whole_spec(taps.shape)] + [block_spec(width)] * 4,
        out_specs=[block_spec(width), block_spec(width), whole_spec(taps.shape)],
        out_shape=[
            jax.ShapeDtypeStruct(q.shape, BF),
            jax.ShapeDtypeStruct(q.shape, BF),
            jax.ShapeDtypeStruct(taps.shape, F32),
        ],
        scratch_shapes=[
            pltpu.VMEM((groups, LANES, LANES), BF),
            pltpu.VMEM((groups, LANES, LANES), F32),
        ],
        compiler_params=PARAMS,
        cost_estimate=pl.CostEstimate(flops=flops, bytes_accessed=12 * q.size, transcendentals=0),
    )(off, taps, q, cot, product, halo)


def seq_pairs(by, turn):
    halves = lax.axis_size("z_hi")
    zeros = lax.axis_size(ZERO)
    pairs = []
    for h in range(halves):
        for z in range(zeros):
            to = z + by
            h_to = h if 0 <= to < zeros else (h + turn) % halves
            pairs.append((h * zeros + z, h_to * zeros + to % zeros))
    return pairs


def halo_forward(product):
    most = lax.ppermute(product[:-1], SEQ_AX, seq_pairs(1, 0))
    last = lax.ppermute(product[-1:], SEQ_AX, seq_pairs(1, 1))
    first = lax.axis_index(ZERO) == 0
    return jnp.where(first, jnp.concatenate([last, most], 0), jnp.concatenate([most, last], 0))


def halo_back(grad_prev):
    first = lax.axis_index(ZERO) == 0
    most = jnp.where(first, grad_prev[1:], grad_prev[:-1])
    last = jnp.where(first, grad_prev[:1], grad_prev[-1:])
    most = lax.ppermute(most, SEQ_AX, seq_pairs(-1, 0))
    last = lax.ppermute(last, SEQ_AX, seq_pairs(-1, -1))
    return jnp.concatenate([most, last], 0)


def body(tokens, in_weight, filters, doc_offset, cotangent):
    hi, lo, xs = lax.axis_size("z_hi"), lax.axis_size("z_lo"), lax.axis_size("x")
    blocks = lax.axis_size(TOK_AX)
    rows = tokens.shape[0]
    feats, width = in_weight.shape[1:]
    wide = hi * width
    by_z = spread(in_weight, Z_AX)
    by_x = spread(by_z, "x")
    by_x = by_x.reshape(xs, hi, lo, 3, feats, width)
    weight = by_x.transpose(2, 0, 4, 3, 1, 5).reshape(lo * xs * feats, 3 * wide)
    gathered = lax.all_gather(tokens, TOK_AX, axis=0, tiled=True)
    cot = cotangent.reshape(rows, hi, blocks, width).transpose(2, 0, 1, 3).reshape(blocks, rows, wide)
    cot = swap_blocks(cot, TOK_AX)
    other = lax.ppermute(filters, "z_hi", [(i, hi - 1 - i) for i in range(hi)])
    upper = lax.axis_index("z_hi") == 0
    taps = jnp.where(upper, jnp.concatenate([filters, other], 0), jnp.concatenate([other, filters], 0))
    taps_back = jnp.roll(jnp.flip(taps, 1), 1, axis=1)
    off = lax.dynamic_slice_in_dim(doc_offset, lax.axis_index("z_hi") * blocks, blocks, 0)[:, None, :]

    projected = jnp.dot(gathered, weight, preferred_element_type=F32).astype(BF)
    projected = projected.reshape(blocks, rows, 3, wide)
    q, k, v = projected[:, :, 0], projected[:, :, 1], projected[:, :, 2]
    product = (k.astype(F32) * v.astype(F32)).astype(BF)
    halo = halo_forward(product)
    grad_prev, grad_own = back(off, taps, q, cot)
    received = halo_back(grad_prev)
    gated, grad_q, grad_taps = front(off, taps_back, q, cot, product, halo)

    out = swap_blocks(gated, TOK_AX)
    out = out.reshape(blocks, rows, hi, width).transpose(1, 2, 0, 3).reshape(rows, -1)

    grad_product = grad_own + received.astype(F32)
    grad_k = (grad_product * v.astype(F32)).astype(BF)
    grad_v = (grad_product * k.astype(F32)).astype(BF)
    grads = jnp.concatenate([grad_q, grad_k, grad_v], 2).reshape(blocks * rows, 3 * wide)
    partial = lax.dot_general(gathered, grads, (((0,), (0,)), ((), ())), preferred_element_type=F32).astype(BF)
    partial = partial.reshape(lo, xs, feats, 3, hi, width).transpose(1, 4, 0, 3, 2, 5)
    over_x = jnp.sum(swap_blocks(partial, "x").astype(F32), 0).astype(BF)
    over_x = over_x.reshape(hi * lo, 3, feats, width)
    grad_weight = jnp.sum(swap_blocks(over_x, Z_AX).astype(F32), 0)

    grad_taps = jnp.roll(jnp.flip(grad_taps, 1), 1, axis=1)
    grad_taps = jnp.sum(spread(grad_taps, "x"), 0).reshape(hi, 1, -1, LANES)
    grad_taps = jnp.broadcast_to(grad_taps, (hi, lo) + grad_taps.shape[2:])
    grad_taps = jnp.sum(swap_blocks(grad_taps.reshape(hi * lo, -1, LANES), Z_AX), 0)
    return (out, grad_weight, grad_taps)


def sharded(mesh):
    return jax.shard_map(
        body,
        mesh=mesh,
        in_specs=(P(CTX + ZERO, None), P(None, ZERO, CTX), P(CTX, None), P(None, ZERO), P(CTX + ZERO, None)),
        out_specs=(P(CTX + ZERO, None), P(None, ZERO, CTX), P(CTX, None)),
        check_vma=False,
    )


def solution(mesh):
    return sharded(Mesh(mesh.devices.reshape(2, 4, 2, 8, 4), CTX + ZERO))
```

```python
import jax
import jax.numpy as jnp
from jax import lax
from jax.experimental import pallas as pl
from jax.experimental.pallas import tpu as pltpu
from jax.sharding import Mesh, PartitionSpec as P

BF = jnp.bfloat16
F32 = jnp.float32
LANES = 128
HALF = 64
GSIZE = 16
PER = LANES // GSIZE
EXTRA = 16
CTX = ("z_hi", "y", "core")
ZERO = ("z_p", "z_c", "x")
TOK_AX = ("y", "core", "z_c")
Z_AX = ("z_hi", "z_p", "z_c")
SEQ_AX = ("z_hi", "z_p", "x")


def swap_blocks(pieces, axes):
    return lax.all_to_all(pieces, axes, split_axis=0, concat_axis=0, tiled=True)


def turned(shard, axis, by):
    count = lax.axis_size(axis)
    return lax.ppermute(shard, axis, [(i, (i + by) % count) for i in range(count)])


def iotas():
    rows = lax.broadcasted_iota(jnp.int32, (LANES, LANES), 0)
    cols = lax.broadcasted_iota(jnp.int32, (LANES, LANES), 1)
    return rows, cols


def group_lanes(block, g):
    lane = lax.broadcasted_iota(jnp.int32, block.shape, 1)
    return jnp.where(lane // GSIZE == g, block, jnp.zeros_like(block))


def lane_halves(first, second):
    low = lax.broadcasted_iota(jnp.int32, first.shape, 1) < HALF
    return (
        jnp.where(low, first, pltpu.roll(second, HALF, 1)),
        jnp.where(low, pltpu.roll(first, HALF, 1), second),
    )


def circulants(taps_ref, table_ref):
    for g in range(taps_ref.shape[0]):
        rows = jnp.broadcast_to(taps_ref[g : g + 1, :], (LANES, LANES))
        table_ref[g] = pltpu.roll(rows, 0, 1, stride=1, stride_axis=0).astype(BF)


def project_kernel(x_ref, tok_ref, *refs):
    w_refs, (q_ref, k_ref, v_ref, prod_ref, table) = refs[:-5], refs[-5:]
    hi, lo, parts, short, _ = w_refs[0].shape
    xs = len(w_refs)

    @pl.when(pl.program_id(0) == 0)
    def _():
        for step, w_ref in enumerate(w_refs):
            x = lax.rem(x_ref[0] - step + xs, xs)
            for l in range(lo):
                at = pl.multiple_of((l * xs + x) * (2 * short), 2 * short)
                for p in range(parts):
                    cols = slice(p * LANES, (p + 1) * LANES)
                    top, low = lane_halves(w_ref[0, l, p].astype(F32), w_ref[1, l, p].astype(F32))
                    table[pl.ds(at, short), cols] = top.astype(BF)
                    table[pl.ds(at + short, short), cols] = low.astype(BF)

    result = jnp.dot(tok_ref[...], table[...], preferred_element_type=F32).astype(BF)
    count, rows = q_ref.shape[:2]
    q, k, v = [result[:, p * LANES : (p + 1) * LANES] for p in range(parts)]
    product = (k.astype(F32) * v.astype(F32)).astype(BF)
    for ref, side in ((q_ref, q), (k_ref, k), (v_ref, v), (prod_ref, product)):
        for j in range(count):
            ref[j] = side[j * rows : (j + 1) * rows]


def back_kernel(off_ref, taps_ref, q_ref, cot_ref, prev_ref, own_ref, table):
    @pl.when(pl.program_id(0) == 0)
    def _():
        circulants(taps_ref, table)

    u, t = iotas()
    lag = t - u
    for j in range(q_ref.shape[0]):
        off = jnp.broadcast_to(off_ref[j], (LANES, LANES))
        m_own = jnp.where((lag >= 0) & (lag <= off), 1.0, 0.0).astype(BF)
        m_prev = jnp.where((lag < 0) & (lag + LANES <= off), 1.0, 0.0).astype(BF)
        grad = (cot_ref[j].astype(F32) * q_ref[j].astype(F32)).astype(BF)
        right = jnp.concatenate([group_lanes(grad, g) for g in range(PER)], 0)
        prev = jnp.concatenate([table[g] * m_prev for g in range(PER)], 1)
        own = jnp.concatenate([table[g] * m_own for g in range(PER)], 1)
        prev_ref[j] = jnp.dot(prev, right, preferred_element_type=F32).astype(BF)
        own_ref[j] = jnp.dot(own, right, preferred_element_type=F32)


def front_kernel(off_ref, taps_ref, q_ref, cot_ref, prod_ref, halo_ref, gated_ref, gq_ref, df_ref, table, acc):
    step = pl.program_id(0)

    @pl.when(step == 0)
    def _():
        circulants(taps_ref, table)
        acc[...] = jnp.zeros_like(acc)

    t, u = iotas()
    lag = t - u
    for j in range(q_ref.shape[0]):
        off = jnp.broadcast_to(off_ref[j], (LANES, LANES)).T
        is_own = (lag >= 0) & (lag <= off)
        is_prev = (lag < 0) & (lag + LANES <= off)
        m_own = jnp.where(is_own, 1.0, 0.0).astype(BF)
        m_prev = jnp.where(is_prev, 1.0, 0.0).astype(BF)
        q = q_ref[j].astype(F32)
        cot = cot_ref[j].astype(F32)
        grad = (cot * q).astype(BF)
        ext = jnp.concatenate([halo_ref[j], prod_ref[j]], 0)
        right = jnp.concatenate([group_lanes(ext, g) for g in range(PER)], 0)
        left = []
        for g in range(PER):
            left += [table[g] * m_prev, table[g] * m_own]
        mixed = jnp.dot(jnp.concatenate(left, 1), right, preferred_element_type=F32)
        gated_ref[j] = (q * mixed).astype(BF)
        gq_ref[j] = (cot * mixed).astype(BF)
        rows = jnp.concatenate([group_lanes(grad, g) for g in range(PER)], 0)
        sums = lax.dot_general(rows, ext, (((1,), (1,)), ((), ())), preferred_element_type=F32)
        for g in range(PER):
            part = sums[g * LANES : (g + 1) * LANES]
            acc[g] += jnp.where(is_own, part[:, LANES:], jnp.where(is_prev, part[:, :LANES], 0.0))

    @pl.when(step == pl.num_programs(0) - 1)
    def _():
        for g in range(PER):
            lined = acc[g]
            for bit in range(7):
                moved = pltpu.roll(lined, LANES - (1 << bit), 1)
                lined = jnp.where((t >> bit) & 1 == 1, moved, lined)
            df_ref[g : g + 1, :] = jnp.sum(lined, axis=0, keepdims=True)


def weight_kernel(x_ref, tok_ref, gq_ref, own_ref, got_ref, k_ref, v_ref, taps_ref, out_ref, grads):
    blocks, rows, _ = own_ref.shape
    xs, hi = out_ref.shape[:2]
    short = (out_ref.shape[3] - EXTRA) // 3

    @pl.when(pl.program_id(0) == 0)
    def _():
        for j in range(blocks):
            grad = own_ref[j] + got_ref[j].astype(F32)
            at = slice(j * rows, (j + 1) * rows)
            grads[at, :LANES] = gq_ref[j]
            grads[at, LANES : 2 * LANES] = (grad * v_ref[j].astype(F32)).astype(BF)
            grads[at, 2 * LANES :] = (grad * k_ref[j].astype(F32)).astype(BF)

    result = lax.dot_general(tok_ref[...], grads[...], (((0,), (0,)), ((), ())), preferred_element_type=F32)
    for x in range(xs):
        slot = lax.rem(x - x_ref[0] + xs, xs)
        for p in range(3):
            block = result[x * 2 * short : (x + 1) * 2 * short, p * LANES : (p + 1) * LANES]
            for h, piece in enumerate(lane_halves(block[:short], block[short:])):
                out_ref[slot, h, 0, p * short : (p + 1) * short] = piece.astype(BF)
        for h in range(hi):
            out_ref[slot, h, 0, 3 * short :] = taps_ref[h]


def block_spec(count):
    return pl.BlockSpec((count, LANES, LANES), lambda i: (i, 0, 0))


def whole_spec(shape):
    return pl.BlockSpec(shape, lambda i: (0,) * len(shape))


SCALAR = pl.BlockSpec(memory_space=pltpu.SMEM)
PARAMS = pltpu.CompilerParams(dimension_semantics=("arbitrary",), vmem_limit_bytes=48 << 20)


def cost(flops, moved):
    return pl.CostEstimate(flops=flops, bytes_accessed=moved, transcendentals=0)


def project(x, tokens, pieces):
    depth = tokens.shape[1]
    blocks, at_once = tokens.shape[0] // LANES, 2
    return pl.pallas_call(
        project_kernel,
        grid=(blocks // at_once,),
        in_specs=[SCALAR, pl.BlockSpec((at_once * LANES, depth), lambda i: (i, 0))]
        + [whole_spec(piece.shape) for piece in pieces],
        out_specs=[block_spec(at_once)] * 4,
        out_shape=[jax.ShapeDtypeStruct((blocks, LANES, LANES), BF)] * 4,
        scratch_shapes=[pltpu.VMEM((depth, 3 * LANES), BF)],
        compiler_params=PARAMS,
        cost_estimate=cost(2 * tokens.size * 3 * LANES, 2 * tokens.size),
    )(x, tokens, *pieces)


def back(off, taps, q, cot):
    n, at_once = q.shape[0], 2
    return pl.pallas_call(
        back_kernel,
        grid=(n // at_once,),
        in_specs=[pl.BlockSpec((at_once, 1, LANES), lambda i: (i, 0, 0)), whole_spec(taps.shape)]
        + [block_spec(at_once)] * 2,
        out_specs=[block_spec(at_once)] * 2,
        out_shape=[jax.ShapeDtypeStruct(q.shape, BF), jax.ShapeDtypeStruct(q.shape, F32)],
        scratch_shapes=[pltpu.VMEM((PER, LANES, LANES), BF)],
        compiler_params=PARAMS,
        cost_estimate=cost(2 * q.size * 2 * LANES * PER, 10 * q.size),
    )(off, taps, q, cot)


def front(off, taps, q, cot, product, halo):
    n, at_once = q.shape[0], 2
    return pl.pallas_call(
        front_kernel,
        grid=(n // at_once,),
        in_specs=[pl.BlockSpec((at_once, 1, LANES), lambda i: (i, 0, 0)), whole_spec(taps.shape)]
        + [block_spec(at_once)] * 4,
        out_specs=[block_spec(at_once)] * 2 + [whole_spec(taps.shape)],
        out_shape=[jax.ShapeDtypeStruct(q.shape, BF)] * 2 + [jax.ShapeDtypeStruct(taps.shape, F32)],
        scratch_shapes=[pltpu.VMEM((PER, LANES, LANES), BF), pltpu.VMEM((PER, LANES, LANES), F32)],
        compiler_params=PARAMS,
        cost_estimate=cost(4 * q.size * 2 * LANES * PER, 12 * q.size),
    )(off, taps, q, cot, product, halo)


def weight_grad(x, tokens, operands, dims):
    xs, hi, lo, feats = dims
    rows = 3 * feats // 2 + EXTRA
    return pl.pallas_call(
        weight_kernel,
        grid=(lo,),
        in_specs=[SCALAR, pl.BlockSpec((tokens.shape[0], xs * feats), lambda i: (0, i))]
        + [whole_spec(operand.shape) for operand in operands],
        out_specs=pl.BlockSpec((xs, hi, 1, rows, LANES), lambda i: (0, 0, i, 0, 0)),
        out_shape=jax.ShapeDtypeStruct((xs, hi, lo, rows, LANES), BF),
        scratch_shapes=[pltpu.VMEM((tokens.shape[0], 3 * LANES), BF)],
        compiler_params=PARAMS,
        cost_estimate=cost(2 * tokens.size * 3 * LANES, 2 * tokens.size),
    )(x, tokens, *operands)


def seq_pairs(by, turn):
    halves = lax.axis_size("z_hi")
    steps = lax.axis_size(("z_p", "x"))
    pairs = []
    for h in range(halves):
        for i in range(steps):
            to = i + by
            h_to = h if 0 <= to < steps else (h + turn) % halves
            pairs.append((h * steps + i, h_to * steps + to % steps))
    return pairs


def at_start():
    return lax.axis_index(("z_p", "x")) == 0


def at_last_x():
    return lax.axis_index("x") == lax.axis_size("x") - 1


def halo_forward(product):
    pairs = product.reshape(-1, 2, LANES, LANES)
    even, odd = pairs[:, 0], pairs[:, 1]
    far = jnp.where(at_last_x(), odd, even)
    near = jnp.where(at_last_x(), even, odd)
    most = lax.ppermute(far[:-1], SEQ_AX, seq_pairs(1, 0))
    last = lax.ppermute(far[-1:], SEQ_AX, seq_pairs(1, 1))
    near = turned(near, "x", 1)
    far = jnp.where(at_start(), jnp.concatenate([last, most], 0), jnp.concatenate([most, last], 0))
    return jnp.stack([far, near], 1).reshape(product.shape)


def halo_back(grad_prev):
    pairs = grad_prev.reshape(-1, 2, LANES, LANES)
    far, near = pairs[:, 0], pairs[:, 1]
    most = jnp.where(at_start(), far[1:], far[:-1])
    last = jnp.where(at_start(), far[:1], far[-1:])
    most = lax.ppermute(most, SEQ_AX, seq_pairs(-1, 0))
    last = lax.ppermute(last, SEQ_AX, seq_pairs(-1, -1))
    near = turned(near, "x", -1)
    far = jnp.concatenate([most, last], 0)
    even = jnp.where(at_last_x(), near, far)
    odd = jnp.where(at_last_x(), far, near)
    return jnp.stack([even, odd], 1).reshape(grad_prev.shape)


def split_rows(values):
    upper = values.astype(BF)
    lower = (values - upper.astype(F32)).astype(BF)
    return jnp.concatenate([upper, lower], -2)


def body(tokens, in_weight, filters, doc_offset, cotangent):
    hi, xs = lax.axis_size("z_hi"), lax.axis_size("x")
    lo = lax.axis_size(("z_p", "z_c"))
    blocks = lax.axis_size(TOK_AX)
    places = blocks // 2
    rows = tokens.shape[0]
    feats, width = in_weight.shape[1:]
    short = feats // 2
    row_count = 3 * short
    x = lax.axis_index("x").astype(jnp.int32)[None]
    member = lax.axis_index("z_c")

    gathered = lax.all_gather(tokens, TOK_AX, axis=0, tiled=True)
    packed = in_weight.reshape(3, 2, short, 2, HALF).transpose(3, 0, 2, 1, 4).reshape(2, row_count, LANES)
    packed = jnp.broadcast_to(packed[None, None], (hi, lo // 2, 2, row_count, LANES))
    by_z = swap_blocks(packed.reshape(hi * lo, row_count, LANES), Z_AX)
    pieces = [by_z] + [turned(by_z, "x", step) for step in range(1, xs)]
    pieces = [piece.reshape(hi, lo, 3, short, LANES) for piece in pieces]
    cot = cotangent.reshape(rows, hi, places, 2, HALF).transpose(2, 3, 0, 1, 4).reshape(blocks, rows, LANES)
    cot = swap_blocks(cot, TOK_AX)

    other = turned(filters, "z_hi", 1)
    upper = lax.axis_index("z_hi") == 0
    taps = jnp.where(upper, jnp.stack([filters, other]), jnp.stack([other, filters]))
    taps = lax.dynamic_slice_in_dim(taps, member * (PER // 2), PER // 2, 1).reshape(PER, LANES)
    taps_back = jnp.roll(jnp.flip(taps, 1), 1, axis=1)
    off = lax.dynamic_slice_in_dim(doc_offset, lax.axis_index("z_hi") * places, places, 0)
    off_other = turned(off, "z_c", 1)
    off = jnp.where(member == 0, jnp.stack([off, off_other], 1), jnp.stack([off_other, off], 1))
    off = off.reshape(blocks, 1, LANES)

    q, k, v, product = project(x, gathered, pieces)
    halo = halo_forward(product)
    grad_prev, grad_own = back(off, taps, q, cot)
    got = halo_back(grad_prev)
    gated, grad_q, grad_taps = front(off, taps_back, q, cot, product, halo)
    out = swap_blocks(gated, TOK_AX)
    out = out.reshape(places, 2, rows, hi, HALF).transpose(2, 3, 0, 1, 4).reshape(rows, -1)

    grad_taps = split_rows(grad_taps.reshape(hi, PER // 2, LANES))
    grad_taps = jnp.pad(grad_taps, ((0, 0), (0, EXTRA - PER), (0, 0)))
    partial = weight_grad(x, gathered, (grad_q, grad_own, got, k, v, grad_taps), (xs, hi, lo, feats))
    parts = [partial[0]] + [turned(partial[step], "x", step) for step in range(1, xs)]
    over_x = sum(part.astype(F32) for part in parts)
    taps_x = over_x[:, :, row_count : row_count + PER // 2] + over_x[:, :, row_count + PER // 2 : row_count + PER]
    taps_x = jnp.pad(split_rows(taps_x), ((0, 0), (0, 0), (0, EXTRA - PER), (0, 0)))
    over_x = jnp.concatenate([over_x[:, :, :row_count].astype(BF), taps_x], 2)
    over_z = swap_blocks(over_x.reshape(hi * lo, row_count + EXTRA, LANES), Z_AX)
    over_z = jnp.sum(over_z.reshape(hi * lo // 2, 2, row_count + EXTRA, LANES).astype(F32), 0)
    grad_weight = over_z[:, :row_count].reshape(2, 3, short, 2, HALF).transpose(1, 3, 2, 0, 4)
    grad_weight = grad_weight.reshape(3, feats, width)
    grad_taps = over_z[:, row_count : row_count + PER // 2] + over_z[:, row_count + PER // 2 : row_count + PER]
    grad_taps = jnp.roll(jnp.flip(grad_taps.reshape(PER, LANES), 1), 1, axis=1)
    return (out, grad_weight, grad_taps)


def sharded(mesh):
    return jax.shard_map(
        body,
        mesh=mesh,
        in_specs=(P(CTX + ZERO, None), P(None, ZERO, CTX), P(CTX, None), P(None, ZERO), P(CTX + ZERO, None)),
        out_specs=(P(CTX + ZERO, None), P(None, ZERO, CTX), P(CTX, None)),
        check_vma=False,
    )


def solution(mesh):
    return sharded(Mesh(mesh.devices.reshape(2, 4, 2, 4, 2, 4), CTX + ZERO))
```

```python
import jax
import jax.numpy as jnp
from jax import lax
from jax.experimental import pallas as pl
from jax.experimental.pallas import tpu as pltpu
from jax.sharding import Mesh, PartitionSpec as P

BF = jnp.bfloat16
F32 = jnp.float32
LANES = 128
HALF = 64
GSIZE = 16
PER = LANES // GSIZE
EXTRA = 16
CTX = ("z_hi", "y", "core")
ZERO = ("z_p", "z_c", "x")
TOK_AX = ("y", "core", "z_c")
Z_AX = ("z_hi", "z_p", "z_c")
SEQ_AX = ("z_hi", "z_p", "x")


def swap_blocks(pieces, axes):
    return lax.all_to_all(pieces, axes, split_axis=0, concat_axis=0, tiled=True)


def turned(shard, axis, by):
    count = lax.axis_size(axis)
    return lax.ppermute(shard, axis, [(i, (i + by) % count) for i in range(count)])


def iotas():
    rows = lax.broadcasted_iota(jnp.int32, (LANES, LANES), 0)
    cols = lax.broadcasted_iota(jnp.int32, (LANES, LANES), 1)
    return rows, cols


def group_lanes(block, g):
    lane = lax.broadcasted_iota(jnp.int32, block.shape, 1)
    return jnp.where(lane // GSIZE == g, block, jnp.zeros_like(block))


def lane_halves(first, second):
    low = lax.broadcasted_iota(jnp.int32, first.shape, 1) < HALF
    return (
        jnp.where(low, first, pltpu.roll(second, HALF, 1)),
        jnp.where(low, pltpu.roll(first, HALF, 1), second),
    )


def circulants(taps_ref, table_ref):
    for g in range(taps_ref.shape[0]):
        rows = jnp.broadcast_to(taps_ref[g : g + 1, :], (LANES, LANES))
        table_ref[g] = pltpu.roll(rows, 0, 1, stride=1, stride_axis=0).astype(BF)


def unpack_kernel(x_ref, *refs):
    w_refs, table = refs[:-1], refs[-1]
    _, lo, parts, short, _ = w_refs[0].shape
    xs = len(w_refs)
    for step, w_ref in enumerate(w_refs):
        x = lax.rem(x_ref[0] - step + xs, xs)
        for l in range(lo):
            at = pl.multiple_of((l * xs + x) * (2 * short), 2 * short)
            for p in range(parts):
                cols = slice(p * LANES, (p + 1) * LANES)
                top, low = lane_halves(w_ref[0, l, p].astype(F32), w_ref[1, l, p].astype(F32))
                table[pl.ds(at, short), cols] = top.astype(BF)
                table[pl.ds(at + short, short), cols] = low.astype(BF)


def project_kernel(off_ref, taps_ref, tok_ref, w_ref, cot_ref, q_ref, k_ref, v_ref, prod_ref, prev_ref, own_ref, table):
    @pl.when(pl.program_id(0) == 0)
    def _():
        circulants(taps_ref, table)

    count, rows = q_ref.shape[:2]
    result = jnp.dot(tok_ref[...], w_ref[...], preferred_element_type=F32).astype(BF)
    u, t = iotas()
    lag = t - u
    for j in range(count):
        q, k, v = [result[j * rows : (j + 1) * rows, p * LANES : (p + 1) * LANES] for p in range(3)]
        q_ref[j] = q
        k_ref[j] = k
        v_ref[j] = v
        prod_ref[j] = (k.astype(F32) * v.astype(F32)).astype(BF)
        off = jnp.broadcast_to(off_ref[j], (LANES, LANES))
        m_own = jnp.where((lag >= 0) & (lag <= off), 1.0, 0.0).astype(BF)
        m_prev = jnp.where((lag < 0) & (lag + LANES <= off), 1.0, 0.0).astype(BF)
        grad = (cot_ref[j].astype(F32) * q.astype(F32)).astype(BF)
        right = jnp.concatenate([group_lanes(grad, g) for g in range(PER)], 0)
        prev = jnp.concatenate([table[g] * m_prev for g in range(PER)], 1)
        own = jnp.concatenate([table[g] * m_own for g in range(PER)], 1)
        prev_ref[j] = jnp.dot(prev, right, preferred_element_type=F32).astype(BF)
        own_ref[j] = jnp.dot(own, right, preferred_element_type=F32)


def front_kernel(off_ref, taps_ref, q_ref, cot_ref, prod_ref, halo_ref, gated_ref, gq_ref, df_ref, table, acc):
    step = pl.program_id(0)

    @pl.when(step == 0)
    def _():
        circulants(taps_ref, table)
        acc[...] = jnp.zeros_like(acc)

    t, u = iotas()
    lag = t - u
    for j in range(q_ref.shape[0]):
        off = jnp.broadcast_to(off_ref[j], (LANES, LANES)).T
        is_own = (lag >= 0) & (lag <= off)
        is_prev = (lag < 0) & (lag + LANES <= off)
        m_own = jnp.where(is_own, 1.0, 0.0).astype(BF)
        m_prev = jnp.where(is_prev, 1.0, 0.0).astype(BF)
        q = q_ref[j].astype(F32)
        cot = cot_ref[j].astype(F32)
        grad = (cot * q).astype(BF)
        ext = jnp.concatenate([halo_ref[j], prod_ref[j]], 0)
        right = jnp.concatenate([group_lanes(ext, g) for g in range(PER)], 0)
        left = []
        for g in range(PER):
            left += [table[g] * m_prev, table[g] * m_own]
        mixed = jnp.dot(jnp.concatenate(left, 1), right, preferred_element_type=F32)
        gated_ref[j] = (q * mixed).astype(BF)
        gq_ref[j] = (cot * mixed).astype(BF)
        rows = jnp.concatenate([group_lanes(grad, g) for g in range(PER)], 0)
        sums = lax.dot_general(rows, ext, (((1,), (1,)), ((), ())), preferred_element_type=F32)
        for g in range(PER):
            part = sums[g * LANES : (g + 1) * LANES]
            acc[g] += jnp.where(is_own, part[:, LANES:], jnp.where(is_prev, part[:, :LANES], 0.0))

    @pl.when(step == pl.num_programs(0) - 1)
    def _():
        for g in range(PER):
            lined = acc[g]
            for bit in range(7):
                moved = pltpu.roll(lined, LANES - (1 << bit), 1)
                lined = jnp.where((t >> bit) & 1 == 1, moved, lined)
            df_ref[g : g + 1, :] = jnp.sum(lined, axis=0, keepdims=True)


def weight_kernel(x_ref, tok_ref, gq_ref, own_ref, got_ref, k_ref, v_ref, taps_ref, out_ref, grads):
    blocks, rows, _ = own_ref.shape
    xs, hi = out_ref.shape[:2]
    short = (out_ref.shape[3] - EXTRA) // 3

    @pl.when(pl.program_id(0) == 0)
    def _():
        for j in range(blocks):
            grad = own_ref[j] + got_ref[j].astype(F32)
            at = slice(j * rows, (j + 1) * rows)
            grads[at, :LANES] = gq_ref[j]
            grads[at, LANES : 2 * LANES] = (grad * v_ref[j].astype(F32)).astype(BF)
            grads[at, 2 * LANES :] = (grad * k_ref[j].astype(F32)).astype(BF)

    result = lax.dot_general(tok_ref[...], grads[...], (((0,), (0,)), ((), ())), preferred_element_type=F32)
    for l in range(out_ref.shape[2]):
        for x in range(xs):
            slot = lax.rem(x - x_ref[0] + xs, xs)
            at = (l * xs + x) * 2 * short
            for p in range(3):
                block = result[at : at + 2 * short, p * LANES : (p + 1) * LANES]
                for h, piece in enumerate(lane_halves(block[:short], block[short:])):
                    out_ref[slot, h, l, p * short : (p + 1) * short] = piece.astype(BF)
            for h in range(hi):
                out_ref[slot, h, l, 3 * short :] = taps_ref[h]


def block_spec(count):
    return pl.BlockSpec((count, LANES, LANES), lambda i: (i, 0, 0))


def whole_spec(shape):
    return pl.BlockSpec(shape, lambda i: (0,) * len(shape))


SCALAR = pl.BlockSpec(memory_space=pltpu.SMEM)
PARAMS = pltpu.CompilerParams(dimension_semantics=("arbitrary",), vmem_limit_bytes=48 << 20)


def cost(flops, moved):
    return pl.CostEstimate(flops=flops, bytes_accessed=moved, transcendentals=0)


def unpack(x, pieces):
    hi, lo, parts, short, _ = pieces[0].shape
    return pl.pallas_call(
        unpack_kernel,
        in_specs=[SCALAR] + [pl.BlockSpec(memory_space=pltpu.VMEM)] * len(pieces),
        out_specs=pl.BlockSpec(memory_space=pltpu.VMEM),
        out_shape=jax.ShapeDtypeStruct((lo * len(pieces) * 2 * short, parts * LANES), BF),
        compiler_params=pltpu.CompilerParams(vmem_limit_bytes=48 << 20),
        cost_estimate=cost(pieces[0].size * 8, pieces[0].size * 16),
    )(x, *pieces)


def project(off, taps, tokens, table, cot):
    depth = tokens.shape[1]
    blocks, at_once = tokens.shape[0] // LANES, 4
    shape = (blocks, LANES, LANES)
    return pl.pallas_call(
        project_kernel,
        grid=(blocks // at_once,),
        in_specs=[
            pl.BlockSpec((at_once, 1, LANES), lambda i: (i, 0, 0)),
            whole_spec(taps.shape),
            pl.BlockSpec((at_once * LANES, depth), lambda i: (i, 0)),
            whole_spec(table.shape),
            block_spec(at_once),
        ],
        out_specs=[block_spec(at_once)] * 6,
        out_shape=[jax.ShapeDtypeStruct(shape, BF)] * 5 + [jax.ShapeDtypeStruct(shape, F32)],
        scratch_shapes=[pltpu.VMEM((PER, LANES, LANES), BF)],
        compiler_params=PARAMS,
        cost_estimate=cost(2 * tokens.size * 3 * LANES + 4 * cot.size * LANES * PER, 2 * tokens.size),
    )(off, taps, tokens, table, cot)


def front(off, taps, q, cot, product, halo):
    n, at_once = q.shape[0], 2
    return pl.pallas_call(
        front_kernel,
        grid=(n // at_once,),
        in_specs=[pl.BlockSpec((at_once, 1, LANES), lambda i: (i, 0, 0)), whole_spec(taps.shape)]
        + [block_spec(at_once)] * 4,
        out_specs=[block_spec(at_once)] * 2 + [whole_spec(taps.shape)],
        out_shape=[jax.ShapeDtypeStruct(q.shape, BF)] * 2 + [jax.ShapeDtypeStruct(taps.shape, F32)],
        scratch_shapes=[pltpu.VMEM((PER, LANES, LANES), BF), pltpu.VMEM((PER, LANES, LANES), F32)],
        compiler_params=PARAMS,
        cost_estimate=cost(4 * q.size * 2 * LANES * PER, 12 * q.size),
    )(off, taps, q, cot, product, halo)


def weight_grad(x, tokens, operands, dims):
    xs, hi, lo, feats = dims
    rows = 3 * feats // 2 + EXTRA
    return pl.pallas_call(
        weight_kernel,
        grid=(lo // 2,),
        in_specs=[SCALAR, pl.BlockSpec((tokens.shape[0], 2 * xs * feats), lambda i: (0, i))]
        + [whole_spec(operand.shape) for operand in operands],
        out_specs=pl.BlockSpec((xs, hi, 2, rows, LANES), lambda i: (0, 0, i, 0, 0)),
        out_shape=jax.ShapeDtypeStruct((xs, hi, lo, rows, LANES), BF),
        scratch_shapes=[pltpu.VMEM((tokens.shape[0], 3 * LANES), BF)],
        compiler_params=PARAMS,
        cost_estimate=cost(2 * tokens.size * 3 * LANES, 2 * tokens.size),
    )(x, tokens, *operands)


def seq_ring(shard, by):
    halves, steps = lax.axis_size("z_hi"), lax.axis_size(("z_p", "x"))
    pairs = [(h * steps + i, h * steps + (i + by) % steps) for h in range(halves) for i in range(steps)]
    return lax.ppermute(shard, SEQ_AX, pairs)


def over_middle(shard):
    halves, steps = lax.axis_size("z_hi"), lax.axis_size(("z_p", "x"))
    ends = [(h * steps + steps - 1, (h + 1) * steps) for h in range(halves - 1)]
    return lax.ppermute(shard, SEQ_AX, ends + [(b, a) for a, b in ends])


def at_start():
    return lax.axis_index(("z_p", "x")) == 0


def at_end():
    return lax.axis_index(("z_p", "x")) == lax.axis_size(("z_p", "x")) - 1


def at_last_x():
    return lax.axis_index("x") == lax.axis_size("x") - 1


def halos(product, grad_prev):
    pairs = product.reshape(-1, 2, LANES, LANES)
    far = jnp.where(at_last_x(), pairs[:, 1], pairs[:, 0])
    near = jnp.where(at_last_x(), pairs[:, 0], pairs[:, 1])
    pairs = grad_prev.reshape(-1, 2, LANES, LANES)
    far_back, near_back = pairs[:, 0], pairs[:, 1]
    last = over_middle(jnp.where(at_start(), far_back[:1], far[-1:]))
    far = seq_ring(far, 1)
    far_back = seq_ring(jnp.where(at_start(), jnp.concatenate([far_back[1:], far_back[:1]], 0), far_back), -1)
    near = turned(near, "x", 1)
    near_back = turned(near_back, "x", -1)
    far = jnp.where(at_start(), jnp.concatenate([last, far[:-1]], 0), far)
    halo = jnp.stack([far, near], 1).reshape(product.shape)
    far_back = jnp.concatenate([far_back[:-1], jnp.where(at_end(), last, far_back[-1:])], 0)
    even = jnp.where(at_last_x(), near_back, far_back)
    odd = jnp.where(at_last_x(), far_back, near_back)
    return halo, jnp.stack([even, odd], 1).reshape(product.shape)


def split_rows(values):
    upper = values.astype(BF)
    lower = (values - upper.astype(F32)).astype(BF)
    return jnp.concatenate([upper, lower], -2)


def body(tokens, in_weight, filters, doc_offset, cotangent):
    hi, xs = lax.axis_size("z_hi"), lax.axis_size("x")
    lo = lax.axis_size(("z_p", "z_c"))
    blocks = lax.axis_size(TOK_AX)
    places = blocks // 2
    rows = tokens.shape[0]
    feats, width = in_weight.shape[1:]
    short = feats // 2
    row_count = 3 * short
    x = lax.axis_index("x").astype(jnp.int32)[None]
    member = lax.axis_index("z_c")

    gathered = lax.all_gather(tokens, TOK_AX, axis=0, tiled=True)
    cot = cotangent.reshape(rows, hi, places, 2, HALF).transpose(2, 3, 0, 1, 4).reshape(blocks, rows, LANES)
    cot = swap_blocks(cot, TOK_AX)
    in_weight, _ = lax.optimization_barrier((in_weight, cot))
    packed = in_weight.reshape(3, 2, short, 2, HALF).transpose(3, 0, 2, 1, 4).reshape(2, row_count, LANES)
    packed = jnp.broadcast_to(packed[None, None], (hi, lo // 2, 2, row_count, LANES))
    by_z = swap_blocks(packed.reshape(hi * lo, row_count, LANES), Z_AX)
    pieces = [by_z] + [turned(by_z, "x", step) for step in range(1, xs)]
    pieces = [piece.reshape(hi, lo, 3, short, LANES) for piece in pieces]
    table = unpack(x, pieces)

    other = turned(filters, "z_hi", 1)
    upper = lax.axis_index("z_hi") == 0
    taps = jnp.where(upper, jnp.stack([filters, other]), jnp.stack([other, filters]))
    taps = lax.dynamic_slice_in_dim(taps, member * (PER // 2), PER // 2, 1).reshape(PER, LANES)
    taps_back = jnp.roll(jnp.flip(taps, 1), 1, axis=1)
    off = lax.dynamic_slice_in_dim(doc_offset, lax.axis_index("z_hi") * places, places, 0)
    off_other = turned(off, "z_c", 1)
    off = jnp.where(member == 0, jnp.stack([off, off_other], 1), jnp.stack([off_other, off], 1))
    off = off.reshape(blocks, 1, LANES)

    q, k, v, product, grad_prev, grad_own = project(off, taps, gathered, table, cot)
    halo, got = halos(product, grad_prev)
    gated, grad_q, grad_taps = front(off, taps_back, q, cot, product, halo)
    out = swap_blocks(gated, TOK_AX)
    out = out.reshape(places, 2, rows, hi, HALF).transpose(2, 3, 0, 1, 4).reshape(rows, -1)

    grad_taps = split_rows(grad_taps.reshape(hi, PER // 2, LANES))
    grad_taps = jnp.pad(grad_taps, ((0, 0), (0, EXTRA - PER), (0, 0)))
    partial = weight_grad(x, gathered, (grad_q, grad_own, got, k, v, grad_taps), (xs, hi, lo, feats))
    parts = [partial[0]] + [turned(partial[step], "x", step) for step in range(1, xs)]
    over_x = sum(part.astype(F32) for part in parts)
    taps_x = over_x[:, :, row_count : row_count + PER // 2] + over_x[:, :, row_count + PER // 2 : row_count + PER]
    taps_x = jnp.pad(split_rows(taps_x), ((0, 0), (0, 0), (0, EXTRA - PER), (0, 0)))
    over_x = jnp.concatenate([over_x[:, :, :row_count].astype(BF), taps_x], 2)
    over_z = swap_blocks(over_x.reshape(hi * lo, row_count + EXTRA, LANES), Z_AX)
    over_z = jnp.sum(over_z.reshape(hi * lo // 2, 2, row_count + EXTRA, LANES).astype(F32), 0)
    grad_weight = over_z[:, :row_count].reshape(2, 3, short, 2, HALF).transpose(1, 3, 2, 0, 4)
    grad_weight = grad_weight.reshape(3, feats, width)
    grad_taps = over_z[:, row_count : row_count + PER // 2] + over_z[:, row_count + PER // 2 : row_count + PER]
    grad_taps = jnp.roll(jnp.flip(grad_taps.reshape(PER, LANES), 1), 1, axis=1)
    return (out, grad_weight, grad_taps)


def sharded(mesh):
    return jax.shard_map(
        body,
        mesh=mesh,
        in_specs=(P(CTX + ZERO, None), P(None, ZERO, CTX), P(CTX, None), P(None, ZERO), P(CTX + ZERO, None)),
        out_specs=(P(CTX + ZERO, None), P(None, ZERO, CTX), P(CTX, None)),
        check_vma=False,
    )


def solution(mesh):
    return sharded(Mesh(mesh.devices.reshape(2, 4, 2, 4, 2, 4), CTX + ZERO))
```

```python
import jax
import jax.numpy as jnp
from jax import lax
from jax.experimental import pallas as pl
from jax.experimental.pallas import tpu as pltpu
from jax.sharding import Mesh, PartitionSpec as P

BF = jnp.bfloat16
F32 = jnp.float32
LANES = 128
HALF = 64
GSIZE = 16
PER = LANES // GSIZE
EXTRA = 16
CTX = ("z_hi", "y", "core")
ZERO = ("z_p", "z_c", "x")
TOK_AX = ("z_c", "y", "core")
Z_AX = ("z_hi", "z_p", "z_c")
SEQ_AX = ("z_hi", "z_p", "x")


def swap_blocks(pieces, axes):
    return lax.all_to_all(pieces, axes, split_axis=0, concat_axis=0, tiled=True)


def turned(shard, axis, by):
    count = lax.axis_size(axis)
    return lax.ppermute(shard, axis, [(i, (i + by) % count) for i in range(count)])


def iotas():
    rows = lax.broadcasted_iota(jnp.int32, (LANES, LANES), 0)
    cols = lax.broadcasted_iota(jnp.int32, (LANES, LANES), 1)
    return rows, cols


def group_lanes(block, g):
    lane = lax.broadcasted_iota(jnp.int32, block.shape, 1)
    return jnp.where(lane // GSIZE == g, block, jnp.zeros_like(block))


def lane_halves(first, second):
    low = lax.broadcasted_iota(jnp.int32, first.shape, 1) < HALF
    return (
        jnp.where(low, first, pltpu.roll(second, HALF, 1)),
        jnp.where(low, pltpu.roll(first, HALF, 1), second),
    )


def circulants(taps_ref, table_ref):
    for g in range(taps_ref.shape[0]):
        rows = jnp.broadcast_to(taps_ref[g : g + 1, :], (LANES, LANES))
        table_ref[g] = pltpu.roll(rows, 0, 1, stride=1, stride_axis=0).astype(BF)


def unpack_kernel(w_ref, table):
    xs, _, lo, parts, short, _ = w_ref.shape
    for x in range(xs):
        for l in range(lo):
            at = (l * xs + x) * (2 * short)
            for p in range(parts):
                cols = slice(p * LANES, (p + 1) * LANES)
                top, low = lane_halves(w_ref[x, 0, l, p].astype(F32), w_ref[x, 1, l, p].astype(F32))
                table[at : at + short, cols] = top.astype(BF)
                table[at + short : at + 2 * short, cols] = low.astype(BF)


def project_kernel(off_ref, taps_ref, tok_ref, w_ref, cot_ref, q_ref, k_ref, v_ref, prod_ref, prev_ref, own_ref, table):
    @pl.when(pl.program_id(0) == 0)
    def _():
        circulants(taps_ref, table)

    count, rows = q_ref.shape[:2]
    result = jnp.dot(tok_ref[...], w_ref[...], preferred_element_type=F32).astype(BF)
    u, t = iotas()
    lag = t - u
    for j in range(count):
        q, k, v = [result[j * rows : (j + 1) * rows, p * LANES : (p + 1) * LANES] for p in range(3)]
        q_ref[j] = q
        k_ref[j] = k
        v_ref[j] = v
        prod_ref[j] = (k.astype(F32) * v.astype(F32)).astype(BF)
        off = jnp.broadcast_to(off_ref[j], (LANES, LANES))
        m_own = jnp.where((lag >= 0) & (lag <= off), 1.0, 0.0).astype(BF)
        m_prev = jnp.where((lag < 0) & (lag + LANES <= off), 1.0, 0.0).astype(BF)
        grad = (cot_ref[j].astype(F32) * q.astype(F32)).astype(BF)
        right = jnp.concatenate([group_lanes(grad, g) for g in range(PER)], 0)
        prev = jnp.concatenate([table[g] * m_prev for g in range(PER)], 1)
        own = jnp.concatenate([table[g] * m_own for g in range(PER)], 1)
        prev_ref[j] = jnp.dot(prev, right, preferred_element_type=F32).astype(BF)
        own_ref[j] = jnp.dot(own, right, preferred_element_type=F32)


def front_kernel(off_ref, taps_ref, q_ref, cot_ref, prod_ref, halo_ref, gated_ref, gq_ref, df_ref, table, acc):
    step = pl.program_id(0)

    @pl.when(step == 0)
    def _():
        circulants(taps_ref, table)
        acc[...] = jnp.zeros_like(acc)

    t, u = iotas()
    lag = t - u
    for j in range(q_ref.shape[0]):
        off = jnp.broadcast_to(off_ref[j], (LANES, LANES)).T
        is_own = (lag >= 0) & (lag <= off)
        is_prev = (lag < 0) & (lag + LANES <= off)
        m_own = jnp.where(is_own, 1.0, 0.0).astype(BF)
        m_prev = jnp.where(is_prev, 1.0, 0.0).astype(BF)
        q = q_ref[j].astype(F32)
        cot = cot_ref[j].astype(F32)
        grad = (cot * q).astype(BF)
        ext = jnp.concatenate([halo_ref[j], prod_ref[j]], 0)
        right = jnp.concatenate([group_lanes(ext, g) for g in range(PER)], 0)
        left = []
        for g in range(PER):
            left += [table[g] * m_prev, table[g] * m_own]
        mixed = jnp.dot(jnp.concatenate(left, 1), right, preferred_element_type=F32)
        gated_ref[j] = (q * mixed).astype(BF)
        gq_ref[j] = (cot * mixed).astype(BF)
        rows = jnp.concatenate([group_lanes(grad, g) for g in range(PER)], 0)
        sums = lax.dot_general(rows, ext, (((1,), (1,)), ((), ())), preferred_element_type=F32)
        for g in range(PER):
            part = sums[g * LANES : (g + 1) * LANES]
            acc[g] += jnp.where(is_own, part[:, LANES:], jnp.where(is_prev, part[:, :LANES], 0.0))

    @pl.when(step == pl.num_programs(0) - 1)
    def _():
        sums = []
        for g in range(PER):
            lined = acc[g]
            for bit in range(7):
                moved = pltpu.roll(lined, LANES - (1 << bit), 1)
                lined = jnp.where((t >> bit) & 1 == 1, moved, lined)
            sums.append(jnp.sum(lined, axis=0, keepdims=True))
        sums = jnp.concatenate(sums, 0)
        upper = sums.astype(BF)
        lower = (sums - upper.astype(F32)).astype(BF)
        mirror = jnp.where((t + u) % LANES == 0, 1.0, 0.0).astype(BF)
        upper = jnp.dot(upper, mirror, preferred_element_type=F32)
        lower = jnp.dot(lower, mirror, preferred_element_type=F32)
        hi = df_ref.shape[0]
        own = PER // hi
        for h in range(hi):
            at = slice(h * own, (h + 1) * own)
            rows = jnp.concatenate([upper[at], lower[at], jnp.zeros((EXTRA - 2 * own, LANES), F32)], 0)
            df_ref[h] = rows.astype(BF)


def weight_kernel(x_ref, tok_ref, gq_ref, own_ref, got_ref, k_ref, v_ref, taps_ref, out_ref, grads):
    blocks, rows, _ = own_ref.shape
    xs, hi = out_ref.shape[:2]
    short = (out_ref.shape[3] - EXTRA) // 3

    @pl.when(pl.program_id(0) == 0)
    def _():
        for j in range(blocks):
            grad = own_ref[j] + got_ref[j].astype(F32)
            at = slice(j * rows, (j + 1) * rows)
            grads[at, :LANES] = gq_ref[j]
            grads[at, LANES : 2 * LANES] = (grad * v_ref[j].astype(F32)).astype(BF)
            grads[at, 2 * LANES :] = (grad * k_ref[j].astype(F32)).astype(BF)

    result = lax.dot_general(tok_ref[...], grads[...], (((0,), (0,)), ((), ())), preferred_element_type=F32)
    for l in range(out_ref.shape[2]):
        for x in range(xs):
            slot = lax.rem(x - x_ref[0] + xs, xs)
            at = (l * xs + x) * 2 * short
            for p in range(3):
                block = result[at : at + 2 * short, p * LANES : (p + 1) * LANES]
                for h, piece in enumerate(lane_halves(block[:short], block[short:])):
                    out_ref[slot, h, l, p * short : (p + 1) * short] = piece.astype(BF)
            for h in range(hi):
                out_ref[slot, h, l, 3 * short :] = taps_ref[h]


def block_spec(count):
    return pl.BlockSpec((count, LANES, LANES), lambda i: (i, 0, 0))


def whole_spec(shape):
    return pl.BlockSpec(shape, lambda i: (0,) * len(shape))


SCALAR = pl.BlockSpec(memory_space=pltpu.SMEM)
PARAMS = pltpu.CompilerParams(dimension_semantics=("arbitrary",), vmem_limit_bytes=48 << 20)


def cost(flops, moved):
    return pl.CostEstimate(flops=flops, bytes_accessed=moved, transcendentals=0)


def unpack(pieces):
    xs, hi, lo, parts, short, _ = pieces.shape
    return pl.pallas_call(
        unpack_kernel,
        in_specs=[pl.BlockSpec(memory_space=pltpu.VMEM)],
        out_specs=pl.BlockSpec(memory_space=pltpu.VMEM),
        out_shape=jax.ShapeDtypeStruct((lo * xs * 2 * short, parts * LANES), BF),
        compiler_params=pltpu.CompilerParams(vmem_limit_bytes=48 << 20),
        cost_estimate=cost(2 * pieces.size, 4 * pieces.size),
    )(pieces)


def project(off, taps, tokens, table, cot):
    depth = tokens.shape[1]
    blocks, at_once = tokens.shape[0] // LANES, 4
    shape = (blocks, LANES, LANES)
    return pl.pallas_call(
        project_kernel,
        grid=(blocks // at_once,),
        in_specs=[
            pl.BlockSpec((at_once, 1, LANES), lambda i: (i, 0, 0)),
            whole_spec(taps.shape),
            pl.BlockSpec((at_once * LANES, depth), lambda i: (i, 0)),
            whole_spec(table.shape),
            block_spec(at_once),
        ],
        out_specs=[block_spec(at_once)] * 6,
        out_shape=[jax.ShapeDtypeStruct(shape, BF)] * 5 + [jax.ShapeDtypeStruct(shape, F32)],
        scratch_shapes=[pltpu.VMEM((PER, LANES, LANES), BF)],
        compiler_params=PARAMS,
        cost_estimate=cost(2 * tokens.size * 3 * LANES + 4 * cot.size * LANES * PER, 2 * tokens.size),
    )(off, taps, tokens, table, cot)


def front(hi, off, taps, q, cot, product, halo):
    n, at_once = q.shape[0], 2
    return pl.pallas_call(
        front_kernel,
        grid=(n // at_once,),
        in_specs=[pl.BlockSpec((at_once, 1, LANES), lambda i: (i, 0, 0)), whole_spec(taps.shape)]
        + [block_spec(at_once)] * 4,
        out_specs=[block_spec(at_once)] * 2 + [whole_spec((hi, EXTRA, LANES))],
        out_shape=[jax.ShapeDtypeStruct(q.shape, BF)] * 2 + [jax.ShapeDtypeStruct((hi, EXTRA, LANES), BF)],
        scratch_shapes=[pltpu.VMEM((PER, LANES, LANES), BF), pltpu.VMEM((PER, LANES, LANES), F32)],
        compiler_params=PARAMS,
        cost_estimate=cost(4 * q.size * 2 * LANES * PER, 12 * q.size),
    )(off, taps, q, cot, product, halo)


def weight_grad(x, tokens, operands, dims):
    xs, hi, lo, feats = dims
    rows = 3 * feats // 2 + EXTRA
    return pl.pallas_call(
        weight_kernel,
        grid=(lo // 2,),
        in_specs=[SCALAR, pl.BlockSpec((tokens.shape[0], 2 * xs * feats), lambda i: (0, i))]
        + [whole_spec(operand.shape) for operand in operands],
        out_specs=pl.BlockSpec((xs, hi, 2, rows, LANES), lambda i: (0, 0, i, 0, 0)),
        out_shape=jax.ShapeDtypeStruct((xs, hi, lo, rows, LANES), BF),
        scratch_shapes=[pltpu.VMEM((tokens.shape[0], 3 * LANES), BF)],
        compiler_params=PARAMS,
        cost_estimate=cost(2 * tokens.size * 3 * LANES, 2 * tokens.size),
    )(x, tokens, *operands)


def seq_ring(shard, by):
    halves, steps = lax.axis_size("z_hi"), lax.axis_size(("z_p", "x"))
    pairs = [(h * steps + i, h * steps + (i + by) % steps) for h in range(halves) for i in range(steps)]
    return lax.ppermute(shard, SEQ_AX, pairs)


def over_middle(shard):
    halves, steps = lax.axis_size("z_hi"), lax.axis_size(("z_p", "x"))
    ends = [(h * steps + steps - 1, (h + 1) * steps) for h in range(halves - 1)]
    return lax.ppermute(shard, SEQ_AX, ends + [(b, a) for a, b in ends])


def at_start():
    return lax.axis_index(("z_p", "x")) == 0


def at_end():
    return lax.axis_index(("z_p", "x")) == lax.axis_size(("z_p", "x")) - 1


def at_last_x():
    return lax.axis_index("x") == lax.axis_size("x") - 1


def halos(product, grad_prev):
    even, odd = product[: product.shape[0] // 2], product[product.shape[0] // 2 :]
    far = jnp.where(at_last_x(), odd, even)
    near = jnp.where(at_last_x(), even, odd)
    far_back, near_back = grad_prev[: even.shape[0]], grad_prev[even.shape[0] :]
    last = over_middle(jnp.where(at_start(), far_back[:1], far[-1:]))
    far = seq_ring(far, 1)
    far_back = seq_ring(jnp.where(at_start(), jnp.concatenate([far_back[1:], far_back[:1]], 0), far_back), -1)
    near = turned(near, "x", 1)
    near_back = turned(near_back, "x", -1)
    far = jnp.where(at_start(), jnp.concatenate([last, far[:-1]], 0), far)
    return jnp.concatenate([far, near], 0), (far_back, near_back, last)


def placed_back(far_back, near_back, last):
    far_back = jnp.concatenate([far_back[:-1], jnp.where(at_end(), last, far_back[-1:])], 0)
    even = jnp.where(at_last_x(), near_back, far_back)
    odd = jnp.where(at_last_x(), far_back, near_back)
    return jnp.concatenate([even, odd], 0)


def split_rows(values):
    upper = values.astype(BF)
    lower = (values - upper.astype(F32)).astype(BF)
    return jnp.concatenate([upper, lower], -2)


def body(tokens, in_weight, filters, doc_offset, cotangent):
    hi, xs = lax.axis_size("z_hi"), lax.axis_size("x")
    lo = lax.axis_size(("z_p", "z_c"))
    blocks = lax.axis_size(TOK_AX)
    places = blocks // 2
    rows = tokens.shape[0]
    feats, width = in_weight.shape[1:]
    short = feats // 2
    row_count = 3 * short
    x = lax.axis_index("x").astype(jnp.int32)[None]
    member = lax.axis_index("z_c")

    gathered = lax.all_gather(tokens, TOK_AX, axis=0, tiled=True)
    packed = in_weight.reshape(3, 2, short, 2, HALF).transpose(3, 0, 2, 1, 4).reshape(2, row_count, LANES)
    packed = jnp.broadcast_to(packed[None, None], (hi, lo // 2, 2, row_count, LANES))
    by_z = swap_blocks(packed.reshape(hi * lo, row_count, LANES), Z_AX)
    other = turned(filters, "z_hi", 1)
    off = lax.dynamic_slice_in_dim(doc_offset, lax.axis_index("z_hi") * places, places, 0)
    off_other = turned(off, "z_c", 1)
    by_z, other, off_other = lax.optimization_barrier((by_z, other, off_other))
    pieces = swap_blocks(jnp.broadcast_to(by_z[None], (xs,) + by_z.shape), "x")
    cotangent, pieces = lax.optimization_barrier((cotangent, pieces))
    cot = cotangent.reshape(rows, hi, places, 2, HALF).transpose(3, 2, 0, 1, 4).reshape(blocks, rows, LANES)
    cot = swap_blocks(cot, TOK_AX)
    table = unpack(pieces.reshape(xs, hi, lo, 3, short, LANES))

    upper = lax.axis_index("z_hi") == 0
    taps = jnp.where(upper, jnp.stack([filters, other]), jnp.stack([other, filters]))
    taps = lax.dynamic_slice_in_dim(taps, member * (PER // 2), PER // 2, 1).reshape(PER, LANES)
    taps_back = jnp.roll(jnp.flip(taps, 1), 1, axis=1)
    off = jnp.where(member == 0, jnp.stack([off, off_other]), jnp.stack([off_other, off]))
    off = off.reshape(blocks, 1, LANES)

    q, k, v, product, grad_prev, grad_own = project(off, taps, gathered, table, cot)
    halo, back = halos(product, grad_prev)
    gated, grad_q, grad_taps = front(hi, off, taps_back, q, cot, product, halo)
    back, grad_q = lax.optimization_barrier((back, grad_q))
    got = placed_back(*back)
    partial = weight_grad(x, gathered, (grad_q, grad_own, got, k, v, grad_taps), (xs, hi, lo, feats))
    gated, partial = lax.optimization_barrier((gated, partial))
    out = swap_blocks(gated, TOK_AX)
    out = out.reshape(2, places, rows, hi, HALF).transpose(2, 3, 1, 0, 4).reshape(rows, -1)
    parts = [partial[0]] + [turned(partial[step], "x", step) for step in range(1, xs)]
    over_x = sum(part.astype(F32) for part in parts)
    taps_x = over_x[:, :, row_count : row_count + PER // 2] + over_x[:, :, row_count + PER // 2 : row_count + PER]
    taps_x = jnp.pad(split_rows(taps_x), ((0, 0), (0, 0), (0, EXTRA - PER), (0, 0)))
    over_x = jnp.concatenate([over_x[:, :, :row_count].astype(BF), taps_x], 2)
    over_z = swap_blocks(over_x.reshape(hi * lo, row_count + EXTRA, LANES), Z_AX)
    over_z = jnp.sum(over_z.reshape(hi * lo // 2, 2, row_count + EXTRA, LANES).astype(F32), 0)
    grad_weight = over_z[:, :row_count].reshape(2, 3, short, 2, HALF).transpose(1, 3, 2, 0, 4)
    grad_weight = grad_weight.reshape(3, feats, width)
    grad_taps = over_z[:, row_count : row_count + PER // 2] + over_z[:, row_count + PER // 2 : row_count + PER]
    grad_taps = grad_taps.reshape(PER, LANES)
    return (out, grad_weight, grad_taps)


def sharded(mesh):
    return jax.shard_map(
        body,
        mesh=mesh,
        in_specs=(P(CTX + ZERO, None), P(None, ZERO, CTX), P(CTX, None), P(None, ZERO), P(CTX + ZERO, None)),
        out_specs=(P(CTX + ZERO, None), P(None, ZERO, CTX), P(CTX, None)),
        check_vma=False,
    )


def solution(mesh):
    return sharded(Mesh(mesh.devices.reshape(2, 4, 2, 4, 2, 4), CTX + ZERO))
```

```python
import jax
import jax.numpy as jnp
from jax import lax
from jax.experimental import pallas as pl
from jax.experimental.pallas import tpu as pltpu
from jax.sharding import Mesh, PartitionSpec as P

BF = jnp.bfloat16
F32 = jnp.float32
LANES = 128
HALF = 64
GSIZE = 16
PER = LANES // GSIZE
EXTRA = 16
CTX = ("z_hi", "y", "core")
ZERO = ("z_p", "z_c", "x")
TOK_AX = ("z_c", "y", "core")
Z_AX = ("z_hi", "z_p", "z_c")
SEQ_AX = ("z_hi", "z_p", "x")


def swap_blocks(pieces, axes):
    return lax.all_to_all(pieces, axes, split_axis=0, concat_axis=0, tiled=True)


def turned(shard, axis, by):
    count = lax.axis_size(axis)
    return lax.ppermute(shard, axis, [(i, (i + by) % count) for i in range(count)])


def iotas():
    rows = lax.broadcasted_iota(jnp.int32, (LANES, LANES), 0)
    cols = lax.broadcasted_iota(jnp.int32, (LANES, LANES), 1)
    return rows, cols


def group_lanes(block, g):
    lane = lax.broadcasted_iota(jnp.int32, block.shape, 1)
    return jnp.where(lane // GSIZE == g, block, jnp.zeros_like(block))


def lane_halves(first, second):
    low = lax.broadcasted_iota(jnp.int32, first.shape, 1) < HALF
    return (
        jnp.where(low, first, pltpu.roll(second, HALF, 1)),
        jnp.where(low, pltpu.roll(first, HALF, 1), second),
    )


def circulants(taps_ref, table_ref):
    for g in range(taps_ref.shape[0]):
        rows = jnp.broadcast_to(taps_ref[g : g + 1, :], (LANES, LANES))
        table_ref[g] = pltpu.roll(rows, 0, 1, stride=1, stride_axis=0).astype(BF)


def unpack_kernel(w_ref, table):
    xs, _, lo, parts, short, _ = w_ref.shape
    for x in range(xs):
        for l in range(lo):
            at = (l * xs + x) * (2 * short)
            for p in range(parts):
                cols = slice(p * LANES, (p + 1) * LANES)
                top, low = lane_halves(w_ref[x, 0, l, p].astype(F32), w_ref[x, 1, l, p].astype(F32))
                table[at : at + short, cols] = top.astype(BF)
                table[at + short : at + 2 * short, cols] = low.astype(BF)


def project_kernel(off_ref, taps_ref, tok_ref, w_ref, cot_ref, q_ref, k_ref, v_ref, prod_ref, prev_ref, own_ref, table):
    @pl.when(pl.program_id(0) == 0)
    def _():
        circulants(taps_ref, table)

    count, rows = q_ref.shape[:2]
    result = jnp.dot(tok_ref[...], w_ref[...], preferred_element_type=F32).astype(BF)
    u, t = iotas()
    lag = t - u
    for j in range(count):
        q, k, v = [result[j * rows : (j + 1) * rows, p * LANES : (p + 1) * LANES] for p in range(3)]
        q_ref[j] = q
        k_ref[j] = k
        v_ref[j] = v
        prod_ref[j] = (k.astype(F32) * v.astype(F32)).astype(BF)
        off = jnp.broadcast_to(off_ref[j], (LANES, LANES))
        m_own = jnp.where((lag >= 0) & (lag <= off), 1.0, 0.0).astype(BF)
        m_prev = jnp.where((lag < 0) & (lag + LANES <= off), 1.0, 0.0).astype(BF)
        grad = (cot_ref[j].astype(F32) * q.astype(F32)).astype(BF)
        right = jnp.concatenate([group_lanes(grad, g) for g in range(PER)], 0)
        prev = jnp.concatenate([table[g] * m_prev for g in range(PER)], 1)
        own = jnp.concatenate([table[g] * m_own for g in range(PER)], 1)
        prev_ref[j] = jnp.dot(prev, right, preferred_element_type=F32).astype(BF)
        own_ref[j] = jnp.dot(own, right, preferred_element_type=F32)


def front_kernel(off_ref, taps_ref, q_ref, cot_ref, prod_ref, halo_ref, gated_ref, gq_ref, df_ref, table, acc):
    step = pl.program_id(0)

    @pl.when(step == 0)
    def _():
        circulants(taps_ref, table)
        acc[...] = jnp.zeros_like(acc)

    t, u = iotas()
    lag = t - u
    for j in range(q_ref.shape[0]):
        off = jnp.broadcast_to(off_ref[j], (LANES, LANES)).T
        is_own = (lag >= 0) & (lag <= off)
        is_prev = (lag < 0) & (lag + LANES <= off)
        m_own = jnp.where(is_own, 1.0, 0.0).astype(BF)
        m_prev = jnp.where(is_prev, 1.0, 0.0).astype(BF)
        q = q_ref[j].astype(F32)
        cot = cot_ref[j].astype(F32)
        grad = (cot * q).astype(BF)
        ext = jnp.concatenate([halo_ref[j], prod_ref[j]], 0)
        right = jnp.concatenate([group_lanes(ext, g) for g in range(PER)], 0)
        left = []
        for g in range(PER):
            left += [table[g] * m_prev, table[g] * m_own]
        mixed = jnp.dot(jnp.concatenate(left, 1), right, preferred_element_type=F32)
        gated_ref[j] = (q * mixed).astype(BF)
        gq_ref[j] = (cot * mixed).astype(BF)
        rows = jnp.concatenate([group_lanes(grad, g) for g in range(PER)], 0)
        sums = lax.dot_general(rows, ext, (((1,), (1,)), ((), ())), preferred_element_type=F32)
        for g in range(PER):
            part = sums[g * LANES : (g + 1) * LANES]
            acc[g] += jnp.where(is_own, part[:, LANES:], jnp.where(is_prev, part[:, :LANES], 0.0))

    @pl.when(step == pl.num_programs(0) - 1)
    def _():
        sums = []
        for g in range(PER):
            lined = acc[g]
            for bit in range(7):
                moved = pltpu.roll(lined, LANES - (1 << bit), 1)
                lined = jnp.where((t >> bit) & 1 == 1, moved, lined)
            sums.append(jnp.sum(lined, axis=0, keepdims=True))
        sums = jnp.concatenate(sums, 0)
        upper = sums.astype(BF)
        lower = (sums - upper.astype(F32)).astype(BF)
        mirror = jnp.where((t + u) % LANES == 0, 1.0, 0.0).astype(BF)
        upper = jnp.dot(upper, mirror, preferred_element_type=F32)
        lower = jnp.dot(lower, mirror, preferred_element_type=F32)
        hi = df_ref.shape[0]
        own = PER // hi
        for h in range(hi):
            at = slice(h * own, (h + 1) * own)
            rows = jnp.concatenate([upper[at], lower[at], jnp.zeros((EXTRA - 2 * own, LANES), F32)], 0)
            df_ref[h] = rows.astype(BF)


def weight_kernel(x_ref, tok_ref, gq_ref, own_ref, got_ref, k_ref, v_ref, taps_ref, out_ref, grads):
    blocks, rows, _ = own_ref.shape
    xs, hi = out_ref.shape[:2]
    short = (out_ref.shape[3] - EXTRA) // 3

    @pl.when(pl.program_id(0) == 0)
    def _():
        for j in range(blocks):
            grad = own_ref[j] + got_ref[j].astype(F32)
            at = slice(j * rows, (j + 1) * rows)
            grads[at, :LANES] = gq_ref[j]
            grads[at, LANES : 2 * LANES] = (grad * v_ref[j].astype(F32)).astype(BF)
            grads[at, 2 * LANES :] = (grad * k_ref[j].astype(F32)).astype(BF)

    result = lax.dot_general(tok_ref[...], grads[...], (((0,), (0,)), ((), ())), preferred_element_type=F32)
    for l in range(out_ref.shape[2]):
        for x in range(xs):
            slot = lax.rem(x - x_ref[0] + xs, xs)
            at = (l * xs + x) * 2 * short
            for p in range(3):
                block = result[at : at + 2 * short, p * LANES : (p + 1) * LANES]
                for h, piece in enumerate(lane_halves(block[:short], block[short:])):
                    out_ref[slot, h, l, p * short : (p + 1) * short] = piece.astype(BF)
            for h in range(hi):
                out_ref[slot, h, l, 3 * short :] = taps_ref[h]


def block_spec(count):
    return pl.BlockSpec((count, LANES, LANES), lambda i: (i, 0, 0))


def whole_spec(shape):
    return pl.BlockSpec(shape, lambda i: (0,) * len(shape))


SCALAR = pl.BlockSpec(memory_space=pltpu.SMEM)
PARAMS = pltpu.CompilerParams(dimension_semantics=("arbitrary",), vmem_limit_bytes=48 << 20)


def cost(flops, moved):
    return pl.CostEstimate(flops=flops, bytes_accessed=moved, transcendentals=0)


def unpack(pieces):
    xs, hi, lo, parts, short, _ = pieces.shape
    return pl.pallas_call(
        unpack_kernel,
        in_specs=[pl.BlockSpec(memory_space=pltpu.VMEM)],
        out_specs=pl.BlockSpec(memory_space=pltpu.VMEM),
        out_shape=jax.ShapeDtypeStruct((lo * xs * 2 * short, parts * LANES), BF),
        compiler_params=pltpu.CompilerParams(vmem_limit_bytes=48 << 20),
        cost_estimate=cost(2 * pieces.size, 4 * pieces.size),
    )(pieces)


def project(off, taps, tokens, table, cot):
    depth = tokens.shape[1]
    blocks, at_once = tokens.shape[0] // LANES, 4
    shape = (blocks, LANES, LANES)
    return pl.pallas_call(
        project_kernel,
        grid=(blocks // at_once,),
        in_specs=[
            pl.BlockSpec((at_once, 1, LANES), lambda i: (i, 0, 0)),
            whole_spec(taps.shape),
            pl.BlockSpec((at_once * LANES, depth), lambda i: (i, 0)),
            whole_spec(table.shape),
            block_spec(at_once),
        ],
        out_specs=[block_spec(at_once)] * 6,
        out_shape=[jax.ShapeDtypeStruct(shape, BF)] * 5 + [jax.ShapeDtypeStruct(shape, F32)],
        scratch_shapes=[pltpu.VMEM((PER, LANES, LANES), BF)],
        compiler_params=PARAMS,
        cost_estimate=cost(2 * tokens.size * 3 * LANES + 4 * cot.size * LANES * PER, 2 * tokens.size),
    )(off, taps, tokens, table, cot)


def front(hi, off, taps, q, cot, product, halo):
    n, at_once = q.shape[0], 4
    return pl.pallas_call(
        front_kernel,
        grid=(n // at_once,),
        in_specs=[pl.BlockSpec((at_once, 1, LANES), lambda i: (i, 0, 0)), whole_spec(taps.shape)]
        + [block_spec(at_once)] * 4,
        out_specs=[block_spec(at_once)] * 2 + [whole_spec((hi, EXTRA, LANES))],
        out_shape=[jax.ShapeDtypeStruct(q.shape, BF)] * 2 + [jax.ShapeDtypeStruct((hi, EXTRA, LANES), BF)],
        scratch_shapes=[pltpu.VMEM((PER, LANES, LANES), BF), pltpu.VMEM((PER, LANES, LANES), F32)],
        compiler_params=PARAMS,
        cost_estimate=cost(4 * q.size * 2 * LANES * PER, 12 * q.size),
    )(off, taps, q, cot, product, halo)


def weight_grad(x, tokens, operands, dims):
    xs, hi, lo, feats = dims
    rows = 3 * feats // 2 + EXTRA
    return pl.pallas_call(
        weight_kernel,
        grid=(lo // 4,),
        in_specs=[SCALAR, pl.BlockSpec((tokens.shape[0], 4 * xs * feats), lambda i: (0, i))]
        + [whole_spec(operand.shape) for operand in operands],
        out_specs=pl.BlockSpec((xs, hi, 4, rows, LANES), lambda i: (0, 0, i, 0, 0)),
        out_shape=jax.ShapeDtypeStruct((xs, hi, lo, rows, LANES), BF),
        scratch_shapes=[pltpu.VMEM((tokens.shape[0], 3 * LANES), BF)],
        compiler_params=PARAMS,
        cost_estimate=cost(2 * tokens.size * 3 * LANES, 2 * tokens.size),
    )(x, tokens, *operands)


def seq_ring(shard, by):
    halves, steps = lax.axis_size("z_hi"), lax.axis_size(("z_p", "x"))
    pairs = [(h * steps + i, h * steps + (i + by) % steps) for h in range(halves) for i in range(steps)]
    return lax.ppermute(shard, SEQ_AX, pairs)


def over_middle(shard):
    halves, steps = lax.axis_size("z_hi"), lax.axis_size(("z_p", "x"))
    ends = [(h * steps + steps - 1, (h + 1) * steps) for h in range(halves - 1)]
    return lax.ppermute(shard, SEQ_AX, ends + [(b, a) for a, b in ends])


def at_start():
    return lax.axis_index(("z_p", "x")) == 0


def at_end():
    return lax.axis_index(("z_p", "x")) == lax.axis_size(("z_p", "x")) - 1


def at_last_x():
    return lax.axis_index("x") == lax.axis_size("x") - 1


def halos(product, grad_prev):
    even, odd = product[: product.shape[0] // 2], product[product.shape[0] // 2 :]
    far = jnp.where(at_last_x(), odd, even)
    near = jnp.where(at_last_x(), even, odd)
    far_back, near_back = grad_prev[: even.shape[0]], grad_prev[even.shape[0] :]
    last = over_middle(jnp.where(at_start(), far_back[:1], far[-1:]))
    far = seq_ring(far, 1)
    far_back = seq_ring(jnp.where(at_start(), jnp.concatenate([far_back[1:], far_back[:1]], 0), far_back), -1)
    near = turned(near, "x", 1)
    near_back = turned(near_back, "x", -1)
    far = jnp.where(at_start(), jnp.concatenate([last, far[:-1]], 0), far)
    return jnp.concatenate([far, near], 0), (far_back, near_back, last)


def placed_back(far_back, near_back, last):
    far_back = jnp.concatenate([far_back[:-1], jnp.where(at_end(), last, far_back[-1:])], 0)
    even = jnp.where(at_last_x(), near_back, far_back)
    odd = jnp.where(at_last_x(), far_back, near_back)
    return jnp.concatenate([even, odd], 0)


def split_rows(values):
    upper = values.astype(BF)
    lower = (values - upper.astype(F32)).astype(BF)
    return jnp.concatenate([upper, lower], -2)


def body(tokens, in_weight, filters, doc_offset, cotangent):
    hi, xs = lax.axis_size("z_hi"), lax.axis_size("x")
    lo = lax.axis_size(("z_p", "z_c"))
    blocks = lax.axis_size(TOK_AX)
    places = blocks // 2
    rows = tokens.shape[0]
    feats, width = in_weight.shape[1:]
    short = feats // 2
    row_count = 3 * short
    x = lax.axis_index("x").astype(jnp.int32)[None]
    member = lax.axis_index("z_c")

    gathered = lax.all_gather(tokens, TOK_AX, axis=0, tiled=True)
    packed = in_weight.reshape(3, 2, short, 2, HALF).transpose(3, 0, 2, 1, 4).reshape(2, row_count, LANES)
    packed = jnp.broadcast_to(packed[None, None], (hi, lo // 2, 2, row_count, LANES))
    by_z = swap_blocks(packed.reshape(hi * lo, row_count, LANES), Z_AX)
    other = turned(filters, "z_hi", 1)
    off = lax.dynamic_slice_in_dim(doc_offset, lax.axis_index("z_hi") * places, places, 0)
    off_other = turned(off, "z_c", 1)
    by_z, other, off_other = lax.optimization_barrier((by_z, other, off_other))
    pieces = swap_blocks(jnp.broadcast_to(by_z[None], (xs,) + by_z.shape), "x")
    cotangent, pieces = lax.optimization_barrier((cotangent, pieces))
    cot = cotangent.reshape(rows, hi, places, 2, HALF).transpose(3, 2, 0, 1, 4).reshape(blocks, rows, LANES)
    cot = swap_blocks(cot, TOK_AX)
    table = unpack(pieces.reshape(xs, hi, lo, 3, short, LANES))

    upper = lax.axis_index("z_hi") == 0
    taps = jnp.where(upper, jnp.stack([filters, other]), jnp.stack([other, filters]))
    taps = lax.dynamic_slice_in_dim(taps, member * (PER // 2), PER // 2, 1).reshape(PER, LANES)
    taps_back = jnp.roll(jnp.flip(taps, 1), 1, axis=1)
    off = jnp.where(member == 0, jnp.stack([off, off_other]), jnp.stack([off_other, off]))
    off = off.reshape(blocks, 1, LANES)

    q, k, v, product, grad_prev, grad_own = project(off, taps, gathered, table, cot)
    halo, back = halos(product, grad_prev)
    gated, grad_q, grad_taps = front(hi, off, taps_back, q, cot, product, halo)
    back, grad_q, gated = lax.optimization_barrier((back, grad_q, gated))
    lower = member == 0
    beside = turned(jnp.where(lower, gated[places:], gated[:places]), "z_c", 1)
    got = placed_back(*back)
    partial = weight_grad(x, gathered, (grad_q, grad_own, got, k, v, grad_taps), (xs, hi, lo, feats))
    beside, partial = lax.optimization_barrier((beside, partial))
    mine = jnp.where(lower, gated[:places], gated[places:])
    both = jnp.where(lower, jnp.stack([mine, beside]), jnp.stack([beside, mine]))
    out = lax.all_gather(both.reshape(blocks * rows, LANES), ("y", "core"), axis=0, tiled=True)
    out = out.reshape(places, 2, places, rows, LANES)
    out = lax.dynamic_index_in_dim(out, lax.axis_index(("y", "core")), 2, keepdims=False)
    out = out.reshape(places, 2, rows, hi, HALF).transpose(2, 3, 0, 1, 4).reshape(rows, -1)
    parts = [partial[0]] + [turned(partial[step], "x", step) for step in range(1, xs)]
    over_x = sum(part.astype(F32) for part in parts)
    taps_x = over_x[:, :, row_count : row_count + PER // 2] + over_x[:, :, row_count + PER // 2 : row_count + PER]
    taps_x = jnp.pad(split_rows(taps_x), ((0, 0), (0, 0), (0, EXTRA - PER), (0, 0)))
    over_x = jnp.concatenate([over_x[:, :, :row_count].astype(BF), taps_x], 2)
    over_z = swap_blocks(over_x.reshape(hi * lo, row_count + EXTRA, LANES), Z_AX)
    over_z, out = lax.optimization_barrier((over_z, out))
    over_z = jnp.sum(over_z.reshape(hi * lo // 2, 2, row_count + EXTRA, LANES).astype(F32), 0)
    grad_weight = over_z[:, :row_count].reshape(2, 3, short, 2, HALF).transpose(1, 3, 2, 0, 4)
    grad_weight = grad_weight.reshape(3, feats, width)
    grad_taps = over_z[:, row_count : row_count + PER // 2] + over_z[:, row_count + PER // 2 : row_count + PER]
    grad_taps = grad_taps.reshape(PER, LANES)
    return (out, grad_weight, grad_taps)


def sharded(mesh):
    return jax.shard_map(
        body,
        mesh=mesh,
        in_specs=(P(CTX + ZERO, None), P(None, ZERO, CTX), P(CTX, None), P(None, ZERO), P(CTX + ZERO, None)),
        out_specs=(P(CTX + ZERO, None), P(None, ZERO, CTX), P(CTX, None)),
        check_vma=False,
    )


def solution(mesh):
    return sharded(Mesh(mesh.devices.reshape(2, 4, 2, 4, 2, 4), CTX + ZERO))
```

```python
import jax
import jax.numpy as jnp
from jax import lax
from jax.experimental import pallas as pl
from jax.experimental.pallas import tpu as pltpu
from jax.sharding import Mesh, PartitionSpec as P

BF = jnp.bfloat16
F32 = jnp.float32
LANES = 128
HALF = 64
GSIZE = 16
PER = LANES // GSIZE
EXTRA = 16
CTX = ("z_hi", "y", "core")
ZERO = ("z_p", "z_c", "x")
TOK_AX = ("z_c", "y", "core")
Z_AX = ("z_hi", "z_p", "z_c")
SEQ_AX = ("z_hi", "z_p", "x")


def swap_blocks(pieces, axes):
    return lax.all_to_all(pieces, axes, split_axis=0, concat_axis=0, tiled=True)


def turned(shard, axis, by):
    count = lax.axis_size(axis)
    return lax.ppermute(shard, axis, [(i, (i + by) % count) for i in range(count)])


def iotas():
    rows = lax.broadcasted_iota(jnp.int32, (LANES, LANES), 0)
    cols = lax.broadcasted_iota(jnp.int32, (LANES, LANES), 1)
    return rows, cols


def group_lanes(block, g):
    lane = lax.broadcasted_iota(jnp.int32, block.shape, 1)
    return jnp.where(lane // GSIZE == g, block, jnp.zeros_like(block))


def lane_halves(first, second):
    low = lax.broadcasted_iota(jnp.int32, first.shape, 1) < HALF
    return (
        jnp.where(low, first, pltpu.roll(second, HALF, 1)),
        jnp.where(low, pltpu.roll(first, HALF, 1), second),
    )


def circulants(taps_ref, table_ref):
    for g in range(taps_ref.shape[0]):
        rows = jnp.broadcast_to(taps_ref[g : g + 1, :], (LANES, LANES))
        table_ref[g] = pltpu.roll(rows, 0, 1, stride=1, stride_axis=0).astype(BF)


def unpack_kernel(x_ref, *refs):
    w_refs, table = refs[:-1], refs[-1]
    _, lo, parts, short, _ = w_refs[0].shape
    xs = len(w_refs)
    for step, w_ref in enumerate(w_refs):
        x = lax.rem(x_ref[0] - step + xs, xs)
        for l in range(lo):
            at = pl.multiple_of((l * xs + x) * (2 * short), 2 * short)
            for p in range(parts):
                cols = slice(p * LANES, (p + 1) * LANES)
                top, low = lane_halves(w_ref[0, l, p].astype(F32), w_ref[1, l, p].astype(F32))
                table[pl.ds(at, short), cols] = top.astype(BF)
                table[pl.ds(at + short, short), cols] = low.astype(BF)


def project_kernel(off_ref, taps_ref, tok_ref, w_ref, cot_ref, q_ref, k_ref, v_ref, prod_ref, prev_ref, own_ref, table):
    @pl.when(pl.program_id(0) == 0)
    def _():
        circulants(taps_ref, table)

    count, rows = q_ref.shape[:2]
    result = jnp.dot(tok_ref[...], w_ref[...], preferred_element_type=F32).astype(BF)
    u, t = iotas()
    lag = t - u
    for j in range(count):
        q, k, v = [result[j * rows : (j + 1) * rows, p * LANES : (p + 1) * LANES] for p in range(3)]
        q_ref[j] = q
        k_ref[j] = k
        v_ref[j] = v
        prod_ref[j] = (k.astype(F32) * v.astype(F32)).astype(BF)
        off = jnp.broadcast_to(off_ref[j], (LANES, LANES))
        m_own = jnp.where((lag >= 0) & (lag <= off), 1.0, 0.0).astype(BF)
        m_prev = jnp.where((lag < 0) & (lag + LANES <= off), 1.0, 0.0).astype(BF)
        grad = (cot_ref[j].astype(F32) * q.astype(F32)).astype(BF)
        right = jnp.concatenate([group_lanes(grad, g) for g in range(PER)], 0)
        prev = jnp.concatenate([table[g] * m_prev for g in range(PER)], 1)
        own = jnp.concatenate([table[g] * m_own for g in range(PER)], 1)
        prev_ref[j] = jnp.dot(prev, right, preferred_element_type=F32).astype(BF)
        own_ref[j] = jnp.dot(own, right, preferred_element_type=F32)


def front_kernel(off_ref, taps_ref, q_ref, cot_ref, prod_ref, halo_ref, gated_ref, gq_ref, df_ref, table, acc):
    step = pl.program_id(0)

    @pl.when(step == 0)
    def _():
        circulants(taps_ref, table)
        acc[...] = jnp.zeros_like(acc)

    t, u = iotas()
    lag = t - u
    for j in range(q_ref.shape[0]):
        off = jnp.broadcast_to(off_ref[j], (LANES, LANES)).T
        is_own = (lag >= 0) & (lag <= off)
        is_prev = (lag < 0) & (lag + LANES <= off)
        m_own = jnp.where(is_own, 1.0, 0.0).astype(BF)
        m_prev = jnp.where(is_prev, 1.0, 0.0).astype(BF)
        q = q_ref[j].astype(F32)
        cot = cot_ref[j].astype(F32)
        grad = (cot * q).astype(BF)
        ext = jnp.concatenate([halo_ref[j], prod_ref[j]], 0)
        right = jnp.concatenate([group_lanes(ext, g) for g in range(PER)], 0)
        left = []
        for g in range(PER):
            left += [table[g] * m_prev, table[g] * m_own]
        mixed = jnp.dot(jnp.concatenate(left, 1), right, preferred_element_type=F32)
        gated_ref[j] = (q * mixed).astype(BF)
        gq_ref[j] = (cot * mixed).astype(BF)
        rows = jnp.concatenate([group_lanes(grad, g) for g in range(PER)], 0)
        sums = lax.dot_general(rows, ext, (((1,), (1,)), ((), ())), preferred_element_type=F32)
        for g in range(PER):
            part = sums[g * LANES : (g + 1) * LANES]
            acc[g] += jnp.where(is_own, part[:, LANES:], jnp.where(is_prev, part[:, :LANES], 0.0))

    @pl.when(step == pl.num_programs(0) - 1)
    def _():
        sums = []
        for g in range(PER):
            lined = acc[g]
            for bit in range(7):
                moved = pltpu.roll(lined, LANES - (1 << bit), 1)
                lined = jnp.where((t >> bit) & 1 == 1, moved, lined)
            sums.append(jnp.sum(lined, axis=0, keepdims=True))
        sums = jnp.concatenate(sums, 0)
        upper = sums.astype(BF)
        lower = (sums - upper.astype(F32)).astype(BF)
        mirror = jnp.where((t + u) % LANES == 0, 1.0, 0.0).astype(BF)
        upper = jnp.dot(upper, mirror, preferred_element_type=F32)
        lower = jnp.dot(lower, mirror, preferred_element_type=F32)
        hi = df_ref.shape[0]
        own = PER // hi
        for h in range(hi):
            at = slice(h * own, (h + 1) * own)
            rows = jnp.concatenate([upper[at], lower[at], jnp.zeros((EXTRA - 2 * own, LANES), F32)], 0)
            df_ref[h] = rows.astype(BF)


def rows_kernel(_, in_ref, out_ref):
    places = in_ref.shape[0]
    for i in range(places):
        sides = lane_halves(in_ref[i, 0, 0].astype(F32), in_ref[i, 1, 0].astype(F32))
        for h, side in enumerate(sides):
            at = (h * places + i) * LANES
            out_ref[:, at : at + LANES] = side.astype(BF)


def weight_kernel(x_ref, tok_ref, gq_ref, own_ref, got_ref, k_ref, v_ref, taps_ref, out_ref, grads):
    blocks, rows, _ = own_ref.shape
    xs, hi = out_ref.shape[:2]
    short = (out_ref.shape[3] - EXTRA) // 3

    @pl.when(pl.program_id(0) == 0)
    def _():
        for j in range(blocks):
            grad = own_ref[j] + got_ref[j].astype(F32)
            at = slice(j * rows, (j + 1) * rows)
            grads[at, :LANES] = gq_ref[j]
            grads[at, LANES : 2 * LANES] = (grad * v_ref[j].astype(F32)).astype(BF)
            grads[at, 2 * LANES :] = (grad * k_ref[j].astype(F32)).astype(BF)

    result = lax.dot_general(tok_ref[...], grads[...], (((0,), (0,)), ((), ())), preferred_element_type=F32)
    for l in range(out_ref.shape[2]):
        for x in range(xs):
            slot = lax.rem(x - x_ref[0] + xs, xs)
            at = (l * xs + x) * 2 * short
            for p in range(3):
                block = result[at : at + 2 * short, p * LANES : (p + 1) * LANES]
                for h, piece in enumerate(lane_halves(block[:short], block[short:])):
                    out_ref[slot, h, l, p * short : (p + 1) * short] = piece.astype(BF)
            for h in range(hi):
                out_ref[slot, h, l, 3 * short :] = taps_ref[h]


def block_spec(count):
    return pl.BlockSpec((count, LANES, LANES), lambda i: (i, 0, 0))


def whole_spec(shape):
    return pl.BlockSpec(shape, lambda i: (0,) * len(shape))


SCALAR = pl.BlockSpec(memory_space=pltpu.SMEM)
PARAMS = pltpu.CompilerParams(dimension_semantics=("arbitrary",), vmem_limit_bytes=48 << 20)


def cost(flops, moved):
    return pl.CostEstimate(flops=flops, bytes_accessed=moved, transcendentals=0)


def unpack(x, pieces):
    hi, lo, parts, short, _ = pieces[0].shape
    return pl.pallas_call(
        unpack_kernel,
        in_specs=[SCALAR] + [pl.BlockSpec(memory_space=pltpu.VMEM)] * len(pieces),
        out_specs=pl.BlockSpec(memory_space=pltpu.VMEM),
        out_shape=jax.ShapeDtypeStruct((lo * len(pieces) * 2 * short, parts * LANES), BF),
        compiler_params=pltpu.CompilerParams(vmem_limit_bytes=48 << 20),
        cost_estimate=cost(pieces[0].size * 8, pieces[0].size * 16),
    )(x, *pieces)


def project(off, taps, tokens, table, cot):
    depth = tokens.shape[1]
    blocks, at_once = tokens.shape[0] // LANES, 4
    shape = (blocks, LANES, LANES)
    return pl.pallas_call(
        project_kernel,
        grid=(blocks // at_once,),
        in_specs=[
            pl.BlockSpec((at_once, 1, LANES), lambda i: (i, 0, 0)),
            whole_spec(taps.shape),
            pl.BlockSpec((at_once * LANES, depth), lambda i: (i, 0)),
            whole_spec(table.shape),
            block_spec(at_once),
        ],
        out_specs=[block_spec(at_once)] * 6,
        out_shape=[jax.ShapeDtypeStruct(shape, BF)] * 5 + [jax.ShapeDtypeStruct(shape, F32)],
        scratch_shapes=[pltpu.VMEM((PER, LANES, LANES), BF)],
        compiler_params=PARAMS,
        cost_estimate=cost(2 * tokens.size * 3 * LANES + 4 * cot.size * LANES * PER, 2 * tokens.size),
    )(off, taps, tokens, table, cot)


def front(hi, off, taps, q, cot, product, halo):
    n, at_once = q.shape[0], 4
    return pl.pallas_call(
        front_kernel,
        grid=(n // at_once,),
        in_specs=[pl.BlockSpec((at_once, 1, LANES), lambda i: (i, 0, 0)), whole_spec(taps.shape)]
        + [block_spec(at_once)] * 4,
        out_specs=[block_spec(at_once)] * 2 + [whole_spec((hi, EXTRA, LANES))],
        out_shape=[jax.ShapeDtypeStruct(q.shape, BF)] * 2 + [jax.ShapeDtypeStruct((hi, EXTRA, LANES), BF)],
        scratch_shapes=[pltpu.VMEM((PER, LANES, LANES), BF), pltpu.VMEM((PER, LANES, LANES), F32)],
        compiler_params=PARAMS,
        cost_estimate=cost(4 * q.size * 2 * LANES * PER, 12 * q.size),
    )(off, taps, q, cot, product, halo)


def output_rows(mine, gathered):
    places, two, _, rows, _ = gathered.shape
    return pl.pallas_call(
        rows_kernel,
        grid_spec=pltpu.PrefetchScalarGridSpec(
            num_scalar_prefetch=1,
            grid=(1,),
            in_specs=[pl.BlockSpec((places, two, 1, rows, LANES), lambda i, mine: (0, 0, mine[0], 0, 0))],
            out_specs=pl.BlockSpec((rows, places * two * LANES), lambda i, mine: (0, 0)),
        ),
        out_shape=jax.ShapeDtypeStruct((rows, places * two * LANES), BF),
        compiler_params=PARAMS,
        cost_estimate=cost(rows * places * two * LANES, 4 * rows * places * two * LANES),
    )(mine, gathered)


def weight_grad(x, tokens, operands, dims):
    xs, hi, lo, feats = dims
    rows = 3 * feats // 2 + EXTRA
    return pl.pallas_call(
        weight_kernel,
        grid=(lo // 4,),
        in_specs=[SCALAR, pl.BlockSpec((tokens.shape[0], 4 * xs * feats), lambda i: (0, i))]
        + [whole_spec(operand.shape) for operand in operands],
        out_specs=pl.BlockSpec((xs, hi, 4, rows, LANES), lambda i: (0, 0, i, 0, 0)),
        out_shape=jax.ShapeDtypeStruct((xs, hi, lo, rows, LANES), BF),
        scratch_shapes=[pltpu.VMEM((tokens.shape[0], 3 * LANES), BF)],
        compiler_params=PARAMS,
        cost_estimate=cost(2 * tokens.size * 3 * LANES, 2 * tokens.size),
    )(x, tokens, *operands)


def seq_ring(shard, by):
    halves, steps = lax.axis_size("z_hi"), lax.axis_size(("z_p", "x"))
    pairs = [(h * steps + i, h * steps + (i + by) % steps) for h in range(halves) for i in range(steps)]
    return lax.ppermute(shard, SEQ_AX, pairs)


def over_middle(shard):
    halves, steps = lax.axis_size("z_hi"), lax.axis_size(("z_p", "x"))
    ends = [(h * steps + steps - 1, (h + 1) * steps) for h in range(halves - 1)]
    return lax.ppermute(shard, SEQ_AX, ends + [(b, a) for a, b in ends])


def at_start():
    return lax.axis_index(("z_p", "x")) == 0


def at_end():
    return lax.axis_index(("z_p", "x")) == lax.axis_size(("z_p", "x")) - 1


def at_last_x():
    return lax.axis_index("x") == lax.axis_size("x") - 1


def halos(product, grad_prev):
    even, odd = product[: product.shape[0] // 2], product[product.shape[0] // 2 :]
    far = jnp.where(at_last_x(), odd, even)
    near = jnp.where(at_last_x(), even, odd)
    far_back, near_back = grad_prev[: even.shape[0]], grad_prev[even.shape[0] :]
    last = over_middle(jnp.where(at_start(), far_back[:1], far[-1:]))
    far = seq_ring(far, 1)
    far_back = seq_ring(jnp.where(at_start(), jnp.concatenate([far_back[1:], far_back[:1]], 0), far_back), -1)
    near = turned(near, "x", 1)
    near_back = turned(near_back, "x", -1)
    far = jnp.where(at_start(), jnp.concatenate([last, far[:-1]], 0), far)
    return jnp.concatenate([far, near], 0), (far_back, near_back, last)


def placed_back(far_back, near_back, last):
    far_back = jnp.concatenate([far_back[:-1], jnp.where(at_end(), last, far_back[-1:])], 0)
    even = jnp.where(at_last_x(), near_back, far_back)
    odd = jnp.where(at_last_x(), far_back, near_back)
    return jnp.concatenate([even, odd], 0)


def split_rows(values):
    upper = values.astype(BF)
    lower = (values - upper.astype(F32)).astype(BF)
    return jnp.concatenate([upper, lower], -2)


def body(tokens, in_weight, filters, doc_offset, cotangent):
    hi, xs = lax.axis_size("z_hi"), lax.axis_size("x")
    lo = lax.axis_size(("z_p", "z_c"))
    blocks = lax.axis_size(TOK_AX)
    places = blocks // 2
    rows = tokens.shape[0]
    feats, width = in_weight.shape[1:]
    short = feats // 2
    row_count = 3 * short
    x = lax.axis_index("x").astype(jnp.int32)[None]
    member = lax.axis_index("z_c")

    gathered = lax.all_gather(tokens, TOK_AX, axis=0, tiled=True)
    packed = in_weight.reshape(3, 2, short, 2, HALF).transpose(3, 0, 2, 1, 4).reshape(2, row_count, LANES)
    packed = jnp.broadcast_to(packed[None, None], (hi, lo // 2, 2, row_count, LANES))
    by_z = swap_blocks(packed.reshape(hi * lo, row_count, LANES), Z_AX)
    other = turned(filters, "z_hi", 1)
    off = lax.dynamic_slice_in_dim(doc_offset, lax.axis_index("z_hi") * places, places, 0)
    off_other = turned(off, "z_c", 1)
    by_z, other, off_other = lax.optimization_barrier((by_z, other, off_other))
    cotangent, by_z = lax.optimization_barrier((cotangent, by_z))
    pieces = [by_z] + [turned(by_z, "x", step) for step in range(1, xs)]
    pieces = [piece.reshape(hi, lo, 3, short, LANES) for piece in pieces]
    cot = cotangent.reshape(rows, hi, places, 2, HALF).transpose(3, 2, 0, 1, 4).reshape(blocks, rows, LANES)
    cot = swap_blocks(cot, TOK_AX)
    table = unpack(x, pieces)

    upper = lax.axis_index("z_hi") == 0
    taps = jnp.where(upper, jnp.stack([filters, other]), jnp.stack([other, filters]))
    taps = lax.dynamic_slice_in_dim(taps, member * (PER // 2), PER // 2, 1).reshape(PER, LANES)
    taps_back = jnp.roll(jnp.flip(taps, 1), 1, axis=1)
    off = jnp.where(member == 0, jnp.stack([off, off_other]), jnp.stack([off_other, off]))
    off = off.reshape(blocks, 1, LANES)

    q, k, v, product, grad_prev, grad_own = project(off, taps, gathered, table, cot)
    halo, back = halos(product, grad_prev)
    gated, grad_q, grad_taps = front(hi, off, taps_back, q, cot, product, halo)
    back, grad_q, gated = lax.optimization_barrier((back, grad_q, gated))
    lower = member == 0
    beside = turned(jnp.where(lower, gated[places:], gated[:places]), "z_c", 1)
    got = placed_back(*back)
    partial = weight_grad(x, gathered, (grad_q, grad_own, got, k, v, grad_taps), (xs, hi, lo, feats))
    beside, partial = lax.optimization_barrier((beside, partial))
    mine = jnp.where(lower, gated[:places], gated[places:])
    both = jnp.where(lower, jnp.stack([mine, beside]), jnp.stack([beside, mine]))
    out = lax.all_gather(both.reshape(blocks * rows, LANES), ("y", "core"), axis=0, tiled=True)
    out = out.reshape(places, 2, places, rows, LANES)
    out = output_rows(lax.axis_index(("y", "core")).astype(jnp.int32)[None], out)
    parts = [partial[0]] + [turned(partial[step], "x", step) for step in range(1, xs)]
    over_x = sum(part.astype(F32) for part in parts)
    taps_x = over_x[:, :, row_count : row_count + PER // 2] + over_x[:, :, row_count + PER // 2 : row_count + PER]
    taps_x = jnp.pad(split_rows(taps_x), ((0, 0), (0, 0), (0, EXTRA - PER), (0, 0)))
    over_x = jnp.concatenate([over_x[:, :, :row_count].astype(BF), taps_x], 2)
    over_z = swap_blocks(over_x.reshape(hi * lo, row_count + EXTRA, LANES), Z_AX)
    over_z, out = lax.optimization_barrier((over_z, out))
    over_z = jnp.sum(over_z.reshape(hi * lo // 2, 2, row_count + EXTRA, LANES).astype(F32), 0)
    grad_weight = over_z[:, :row_count].reshape(2, 3, short, 2, HALF).transpose(1, 3, 2, 0, 4)
    grad_weight = grad_weight.reshape(3, feats, width)
    grad_taps = over_z[:, row_count : row_count + PER // 2] + over_z[:, row_count + PER // 2 : row_count + PER]
    grad_taps = grad_taps.reshape(PER, LANES)
    return (out, grad_weight, grad_taps)


def sharded(mesh):
    return jax.shard_map(
        body,
        mesh=mesh,
        in_specs=(P(CTX + ZERO, None), P(None, ZERO, CTX), P(CTX, None), P(None, ZERO), P(CTX + ZERO, None)),
        out_specs=(P(CTX + ZERO, None), P(None, ZERO, CTX), P(CTX, None)),
        check_vma=False,
    )


def solution(mesh):
    return sharded(Mesh(mesh.devices.reshape(2, 4, 2, 4, 2, 4), CTX + ZERO))
```

```python
import jax
import jax.numpy as jnp
from jax import lax
from jax.experimental import pallas as pl
from jax.experimental.pallas import tpu as pltpu
from jax.sharding import Mesh, PartitionSpec as P

BF = jnp.bfloat16
F32 = jnp.float32
LANES = 128
HALF = 64
GSIZE = 16
PER = LANES // GSIZE
EXTRA = 16
CTX = ("z_hi", "y", "core")
ZERO = ("z_p", "z_c", "x")
TOK_AX = ("z_c", "y", "core")
Z_AX = ("z_hi", "z_p", "z_c")
SEQ_AX = ("z_hi", "z_p", "x")


def swap_blocks(pieces, axes):
    return lax.all_to_all(pieces, axes, split_axis=0, concat_axis=0, tiled=True)


def turned(shard, axis, by):
    count = lax.axis_size(axis)
    return lax.ppermute(shard, axis, [(i, (i + by) % count) for i in range(count)])


def iotas():
    rows = lax.broadcasted_iota(jnp.int32, (LANES, LANES), 0)
    cols = lax.broadcasted_iota(jnp.int32, (LANES, LANES), 1)
    return rows, cols


def group_lanes(block, g):
    lane = lax.broadcasted_iota(jnp.int32, block.shape, 1)
    return jnp.where(lane // GSIZE == g, block, jnp.zeros_like(block))


def lane_halves(first, second):
    low = lax.broadcasted_iota(jnp.int32, first.shape, 1) < HALF
    return (
        jnp.where(low, first, pltpu.roll(second, HALF, 1)),
        jnp.where(low, pltpu.roll(first, HALF, 1), second),
    )


def circulants(taps_ref, table_ref):
    for g in range(taps_ref.shape[0]):
        rows = jnp.broadcast_to(taps_ref[g : g + 1, :], (LANES, LANES))
        table_ref[g] = pltpu.roll(rows, 0, 1, stride=1, stride_axis=0).astype(BF)


def unpack_kernel(x_ref, *refs):
    w_refs, table = refs[:-1], refs[-1]
    _, lo, parts, short, _ = w_refs[0].shape
    xs = len(w_refs)
    for step, w_ref in enumerate(w_refs):
        x = lax.rem(x_ref[0] - step + xs, xs)
        for l in range(lo):
            at = pl.multiple_of((l * xs + x) * (2 * short), 2 * short)
            for p in range(parts):
                cols = slice(p * LANES, (p + 1) * LANES)
                top, low = lane_halves(w_ref[0, l, p].astype(F32), w_ref[1, l, p].astype(F32))
                table[pl.ds(at, short), cols] = top.astype(BF)
                table[pl.ds(at + short, short), cols] = low.astype(BF)


def project_kernel(off_ref, taps_ref, tok_ref, w_ref, cot_ref, q_ref, k_ref, v_ref, prod_ref, prev_ref, own_ref, table):
    @pl.when(pl.program_id(0) == 0)
    def _():
        circulants(taps_ref, table)

    count, rows = q_ref.shape[:2]
    result = jnp.dot(tok_ref[...], w_ref[...], preferred_element_type=F32).astype(BF)
    u, t = iotas()
    lag = t - u
    for j in range(count):
        q, k, v = [result[j * rows : (j + 1) * rows, p * LANES : (p + 1) * LANES] for p in range(3)]
        q_ref[j] = q
        k_ref[j] = k
        v_ref[j] = v
        prod_ref[j] = (k.astype(F32) * v.astype(F32)).astype(BF)
        off = jnp.broadcast_to(off_ref[j], (LANES, LANES))
        m_own = jnp.where((lag >= 0) & (lag <= off), 1.0, 0.0).astype(BF)
        m_prev = jnp.where((lag < 0) & (lag + LANES <= off), 1.0, 0.0).astype(BF)
        grad = (cot_ref[j].astype(F32) * q.astype(F32)).astype(BF)
        right = jnp.concatenate([group_lanes(grad, g) for g in range(PER)], 0)
        prev = jnp.concatenate([table[g] * m_prev for g in range(PER)], 1)
        own = jnp.concatenate([table[g] * m_own for g in range(PER)], 1)
        prev_ref[j] = jnp.dot(prev, right, preferred_element_type=F32).astype(BF)
        own_ref[j] = jnp.dot(own, right, preferred_element_type=F32)


def front_kernel(_, off_ref, taps_ref, q_ref, cot_ref, prod_ref, halo_ref, gated_ref, gq_ref, df_ref, table, acc):
    step = pl.program_id(0)

    @pl.when(step == 0)
    def _():
        circulants(taps_ref, table)
        acc[...] = jnp.zeros_like(acc)

    t, u = iotas()
    lag = t - u
    for j in range(q_ref.shape[0]):
        off = jnp.broadcast_to(off_ref[j], (LANES, LANES)).T
        is_own = (lag >= 0) & (lag <= off)
        is_prev = (lag < 0) & (lag + LANES <= off)
        m_own = jnp.where(is_own, 1.0, 0.0).astype(BF)
        m_prev = jnp.where(is_prev, 1.0, 0.0).astype(BF)
        q = q_ref[j].astype(F32)
        cot = cot_ref[j].astype(F32)
        grad = (cot * q).astype(BF)
        ext = jnp.concatenate([halo_ref[j], prod_ref[j]], 0)
        right = jnp.concatenate([group_lanes(ext, g) for g in range(PER)], 0)
        left = []
        for g in range(PER):
            left += [table[g] * m_prev, table[g] * m_own]
        mixed = jnp.dot(jnp.concatenate(left, 1), right, preferred_element_type=F32)
        gated_ref[j] = (q * mixed).astype(BF)
        gq_ref[j] = (cot * mixed).astype(BF)
        rows = jnp.concatenate([group_lanes(grad, g) for g in range(PER)], 0)
        sums = lax.dot_general(rows, ext, (((1,), (1,)), ((), ())), preferred_element_type=F32)
        for g in range(PER):
            part = sums[g * LANES : (g + 1) * LANES]
            acc[g] += jnp.where(is_own, part[:, LANES:], jnp.where(is_prev, part[:, :LANES], 0.0))

    @pl.when(step == pl.num_programs(0) - 1)
    def _():
        sums = []
        for g in range(PER):
            lined = acc[g]
            for bit in range(7):
                moved = pltpu.roll(lined, LANES - (1 << bit), 1)
                lined = jnp.where((t >> bit) & 1 == 1, moved, lined)
            sums.append(jnp.sum(lined, axis=0, keepdims=True))
        sums = jnp.concatenate(sums, 0)
        upper = sums.astype(BF)
        lower = (sums - upper.astype(F32)).astype(BF)
        mirror = jnp.where((t + u) % LANES == 0, 1.0, 0.0).astype(BF)
        upper = jnp.dot(upper, mirror, preferred_element_type=F32)
        lower = jnp.dot(lower, mirror, preferred_element_type=F32)
        hi = df_ref.shape[0]
        own = PER // hi
        for h in range(hi):
            at = slice(h * own, (h + 1) * own)
            rows = jnp.concatenate([upper[at], lower[at], jnp.zeros((EXTRA - 2 * own, LANES), F32)], 0)
            df_ref[h] = rows.astype(BF)


def rows_kernel(mine_ref, in_ref, out_ref):
    places = in_ref.shape[0]
    lower = mine_ref[1] == 0
    for i in range(places):
        own, beside = in_ref[i, 0, 0].astype(F32), in_ref[i, 1, 0].astype(F32)
        sides = lane_halves(jnp.where(lower, own, beside), jnp.where(lower, beside, own))
        for h, side in enumerate(sides):
            at = (h * places + i) * LANES
            out_ref[:, at : at + LANES] = side.astype(BF)


def weight_kernel(x_ref, tok_ref, gq_ref, own_ref, got_ref, k_ref, v_ref, taps_ref, out_ref, grads):
    blocks, rows, _ = own_ref.shape
    xs, hi = out_ref.shape[:2]
    short = (out_ref.shape[3] - EXTRA) // 3

    @pl.when(pl.program_id(0) == 0)
    def _():
        for j in range(blocks):
            grad = own_ref[j] + got_ref[j].astype(F32)
            at = slice(j * rows, (j + 1) * rows)
            grads[at, :LANES] = gq_ref[j]
            grads[at, LANES : 2 * LANES] = (grad * v_ref[j].astype(F32)).astype(BF)
            grads[at, 2 * LANES :] = (grad * k_ref[j].astype(F32)).astype(BF)

    result = lax.dot_general(tok_ref[...], grads[...], (((0,), (0,)), ((), ())), preferred_element_type=F32)
    for l in range(out_ref.shape[2]):
        for x in range(xs):
            slot = lax.rem(x - x_ref[0] + xs, xs)
            at = (l * xs + x) * 2 * short
            for p in range(3):
                block = result[at : at + 2 * short, p * LANES : (p + 1) * LANES]
                for h, piece in enumerate(lane_halves(block[:short], block[short:])):
                    out_ref[slot, h, l, p * short : (p + 1) * short] = piece.astype(BF)
            for h in range(hi):
                out_ref[slot, h, l, 3 * short :] = taps_ref[h]


def block_spec(count):
    return pl.BlockSpec((count, LANES, LANES), lambda i: (i, 0, 0))


def whole_spec(shape):
    return pl.BlockSpec(shape, lambda i: (0,) * len(shape))


SCALAR = pl.BlockSpec(memory_space=pltpu.SMEM)
PARAMS = pltpu.CompilerParams(dimension_semantics=("arbitrary",), vmem_limit_bytes=48 << 20)


def cost(flops, moved):
    return pl.CostEstimate(flops=flops, bytes_accessed=moved, transcendentals=0)


def unpack(x, pieces):
    hi, lo, parts, short, _ = pieces[0].shape
    return pl.pallas_call(
        unpack_kernel,
        in_specs=[SCALAR] + [pl.BlockSpec(memory_space=pltpu.VMEM)] * len(pieces),
        out_specs=pl.BlockSpec(memory_space=pltpu.VMEM),
        out_shape=jax.ShapeDtypeStruct((lo * len(pieces) * 2 * short, parts * LANES), BF),
        compiler_params=pltpu.CompilerParams(vmem_limit_bytes=48 << 20),
        cost_estimate=cost(pieces[0].size * 8, pieces[0].size * 16),
    )(x, *pieces)


def project(off, taps, tokens, table, cot):
    depth = tokens.shape[1]
    blocks, at_once = tokens.shape[0] // LANES, 4
    shape = (blocks, LANES, LANES)
    return pl.pallas_call(
        project_kernel,
        grid=(blocks // at_once,),
        in_specs=[
            pl.BlockSpec((at_once, 1, LANES), lambda i: (i, 0, 0)),
            whole_spec(taps.shape),
            pl.BlockSpec((at_once * LANES, depth), lambda i: (i, 0)),
            whole_spec(table.shape),
            block_spec(at_once),
        ],
        out_specs=[block_spec(at_once)] * 6,
        out_shape=[jax.ShapeDtypeStruct(shape, BF)] * 5 + [jax.ShapeDtypeStruct(shape, F32)],
        scratch_shapes=[pltpu.VMEM((PER, LANES, LANES), BF)],
        compiler_params=PARAMS,
        cost_estimate=cost(2 * tokens.size * 3 * LANES + 4 * cot.size * LANES * PER, 2 * tokens.size),
    )(off, taps, tokens, table, cot)


def front(hi, member, off, taps, q, cot, product, halo):
    n = q.shape[0]
    at_once = min(4, n // 2)
    steps = n // at_once
    block = pl.BlockSpec((at_once, LANES, LANES), lambda i, member: (i, 0, 0))
    shape = (at_once, LANES, LANES)
    own_first = pl.BlockSpec(shape, lambda i, member: (lax.rem(i + member[0] * (steps // 2), steps), 0, 0))
    return pl.pallas_call(
        front_kernel,
        grid_spec=pltpu.PrefetchScalarGridSpec(
            num_scalar_prefetch=1,
            grid=(steps,),
            in_specs=[
                pl.BlockSpec((at_once, 1, LANES), lambda i, member: (i, 0, 0)),
                pl.BlockSpec(taps.shape, lambda i, member: (0, 0)),
            ]
            + [block] * 4,
            out_specs=[own_first, block, pl.BlockSpec((hi, EXTRA, LANES), lambda i, member: (0, 0, 0))],
            scratch_shapes=[pltpu.VMEM((PER, LANES, LANES), BF), pltpu.VMEM((PER, LANES, LANES), F32)],
        ),
        out_shape=[jax.ShapeDtypeStruct(q.shape, BF)] * 2 + [jax.ShapeDtypeStruct((hi, EXTRA, LANES), BF)],
        compiler_params=PARAMS,
        cost_estimate=cost(4 * q.size * 2 * LANES * PER, 12 * q.size),
    )(member, off, taps, q, cot, product, halo)


def output_rows(mine, gathered):
    places, two, _, rows, _ = gathered.shape
    return pl.pallas_call(
        rows_kernel,
        grid_spec=pltpu.PrefetchScalarGridSpec(
            num_scalar_prefetch=1,
            grid=(1,),
            in_specs=[pl.BlockSpec((places, two, 1, rows, LANES), lambda i, mine: (0, 0, mine[0], 0, 0))],
            out_specs=pl.BlockSpec((rows, places * two * LANES), lambda i, mine: (0, 0)),
        ),
        out_shape=jax.ShapeDtypeStruct((rows, places * two * LANES), BF),
        compiler_params=PARAMS,
        cost_estimate=cost(rows * places * two * LANES, 4 * rows * places * two * LANES),
    )(mine, gathered)


def weight_grad(x, tokens, operands, dims):
    xs, hi, lo, feats = dims
    rows = 3 * feats // 2 + EXTRA
    return pl.pallas_call(
        weight_kernel,
        grid=(lo // 4,),
        in_specs=[SCALAR, pl.BlockSpec((tokens.shape[0], 4 * xs * feats), lambda i: (0, i))]
        + [whole_spec(operand.shape) for operand in operands],
        out_specs=pl.BlockSpec((xs, hi, 4, rows, LANES), lambda i: (0, 0, i, 0, 0)),
        out_shape=jax.ShapeDtypeStruct((xs, hi, lo, rows, LANES), BF),
        scratch_shapes=[pltpu.VMEM((tokens.shape[0], 3 * LANES), BF)],
        compiler_params=PARAMS,
        cost_estimate=cost(2 * tokens.size * 3 * LANES, 2 * tokens.size),
    )(x, tokens, *operands)


def seq_ring(shard, by):
    halves, steps = lax.axis_size("z_hi"), lax.axis_size(("z_p", "x"))
    pairs = [(h * steps + i, h * steps + (i + by) % steps) for h in range(halves) for i in range(steps)]
    return lax.ppermute(shard, SEQ_AX, pairs)


def over_middle(shard):
    halves, steps = lax.axis_size("z_hi"), lax.axis_size(("z_p", "x"))
    ends = [(h * steps + steps - 1, (h + 1) * steps) for h in range(halves - 1)]
    return lax.ppermute(shard, SEQ_AX, ends + [(b, a) for a, b in ends])


def at_start():
    return lax.axis_index(("z_p", "x")) == 0


def at_end():
    return lax.axis_index(("z_p", "x")) == lax.axis_size(("z_p", "x")) - 1


def at_last_x():
    return lax.axis_index("x") == lax.axis_size("x") - 1


def halos(product, grad_prev):
    even, odd = product[: product.shape[0] // 2], product[product.shape[0] // 2 :]
    far = jnp.where(at_last_x(), odd, even)
    near = jnp.where(at_last_x(), even, odd)
    far_back, near_back = grad_prev[: even.shape[0]], grad_prev[even.shape[0] :]
    last = over_middle(jnp.where(at_start(), far_back[:1], far[-1:]))
    far = seq_ring(far, 1)
    far_back = seq_ring(jnp.where(at_start(), jnp.concatenate([far_back[1:], far_back[:1]], 0), far_back), -1)
    near = turned(near, "x", 1)
    near_back = turned(near_back, "x", -1)
    far = jnp.where(at_start(), jnp.concatenate([last, far[:-1]], 0), far)
    return jnp.concatenate([far, near], 0), (far_back, near_back, last)


def placed_back(far_back, near_back, last):
    far_back = jnp.concatenate([far_back[:-1], jnp.where(at_end(), last, far_back[-1:])], 0)
    even = jnp.where(at_last_x(), near_back, far_back)
    odd = jnp.where(at_last_x(), far_back, near_back)
    return jnp.concatenate([even, odd], 0)


def split_rows(values):
    upper = values.astype(BF)
    lower = (values - upper.astype(F32)).astype(BF)
    return jnp.concatenate([upper, lower], -2)


def body(tokens, in_weight, filters, doc_offset, cotangent):
    hi, xs = lax.axis_size("z_hi"), lax.axis_size("x")
    lo = lax.axis_size(("z_p", "z_c"))
    blocks = lax.axis_size(TOK_AX)
    places = blocks // 2
    rows = tokens.shape[0]
    feats, width = in_weight.shape[1:]
    short = feats // 2
    row_count = 3 * short
    x = lax.axis_index("x").astype(jnp.int32)[None]
    member = lax.axis_index("z_c")

    gathered = lax.all_gather(tokens, TOK_AX, axis=0, tiled=True)
    packed = in_weight.reshape(3, 2, short, 2, HALF).transpose(3, 0, 2, 1, 4).reshape(2, row_count, LANES)
    packed = jnp.broadcast_to(packed[None, None], (hi, lo // 2, 2, row_count, LANES))
    by_z = swap_blocks(packed.reshape(hi * lo, row_count, LANES), Z_AX)
    other = turned(filters, "z_hi", 1)
    off = lax.dynamic_slice_in_dim(doc_offset, lax.axis_index("z_hi") * places, places, 0)
    off_other = turned(off, "z_c", 1)
    by_z, other, off_other = lax.optimization_barrier((by_z, other, off_other))
    cotangent, by_z = lax.optimization_barrier((cotangent, by_z))
    pieces = [by_z] + [turned(by_z, "x", step) for step in range(1, xs)]
    pieces = [piece.reshape(hi, lo, 3, short, LANES) for piece in pieces]
    cot = cotangent.reshape(rows, hi, places, 2, HALF).transpose(3, 2, 0, 1, 4).reshape(blocks, rows, LANES)
    cot = swap_blocks(cot, TOK_AX)
    table = unpack(x, pieces)

    upper = lax.axis_index("z_hi") == 0
    taps = jnp.where(upper, jnp.stack([filters, other]), jnp.stack([other, filters]))
    taps = lax.dynamic_slice_in_dim(taps, member * (PER // 2), PER // 2, 1).reshape(PER, LANES)
    taps_back = jnp.roll(jnp.flip(taps, 1), 1, axis=1)
    off = jnp.where(member == 0, jnp.stack([off, off_other]), jnp.stack([off_other, off]))
    off = off.reshape(blocks, 1, LANES)

    q, k, v, product, grad_prev, grad_own = project(off, taps, gathered, table, cot)
    halo, back = halos(product, grad_prev)
    gated, grad_q, grad_taps = front(hi, member.astype(jnp.int32)[None], off, taps_back, q, cot, product, halo)
    back, grad_q, gated = lax.optimization_barrier((back, grad_q, gated))
    beside = turned(gated[places:], "z_c", 1)
    got = placed_back(*back)
    partial = weight_grad(x, gathered, (grad_q, grad_own, got, k, v, grad_taps), (xs, hi, lo, feats))
    beside, partial = lax.optimization_barrier((beside, partial))
    both = jnp.concatenate([gated[:places], beside], 0)
    out = lax.all_gather(both.reshape(blocks * rows, LANES), ("y", "core"), axis=0, tiled=True)
    out = out.reshape(places, 2, places, rows, LANES)
    out = output_rows(jnp.stack([lax.axis_index(("y", "core")), member]).astype(jnp.int32), out)
    parts = [partial[0]] + [turned(partial[step], "x", step) for step in range(1, xs)]
    over_x = sum(part.astype(F32) for part in parts)
    taps_x = over_x[:, :, row_count : row_count + PER // 2] + over_x[:, :, row_count + PER // 2 : row_count + PER]
    taps_x = jnp.pad(split_rows(taps_x), ((0, 0), (0, 0), (0, EXTRA - PER), (0, 0)))
    over_x = jnp.concatenate([over_x[:, :, :row_count].astype(BF), taps_x], 2)
    over_z = swap_blocks(over_x.reshape(hi * lo, row_count + EXTRA, LANES), Z_AX)
    over_z, out = lax.optimization_barrier((over_z, out))
    over_z = jnp.sum(over_z.reshape(hi * lo // 2, 2, row_count + EXTRA, LANES).astype(F32), 0)
    grad_weight = over_z[:, :row_count].reshape(2, 3, short, 2, HALF).transpose(1, 3, 2, 0, 4)
    grad_weight = grad_weight.reshape(3, feats, width)
    grad_taps = over_z[:, row_count : row_count + PER // 2] + over_z[:, row_count + PER // 2 : row_count + PER]
    grad_taps = grad_taps.reshape(PER, LANES)
    return (out, grad_weight, grad_taps)


def sharded(mesh):
    return jax.shard_map(
        body,
        mesh=mesh,
        in_specs=(P(CTX + ZERO, None), P(None, ZERO, CTX), P(CTX, None), P(None, ZERO), P(CTX + ZERO, None)),
        out_specs=(P(CTX + ZERO, None), P(None, ZERO, CTX), P(CTX, None)),
        check_vma=False,
    )


def solution(mesh):
    return sharded(Mesh(mesh.devices.reshape(2, 4, 2, 4, 2, 4), CTX + ZERO))
```
